512 devices in a mesh: grp: 16 (over x, y_hi), dev: 32 (over z, y_lo, core).
Axes of the slice: x: 4, y: 8 (y_hi: 4, y_lo: 2; y = y_hi * 2 + y_lo), z: 8, core: 2. Of those that a mesh axis runs over, the one named last changes fastest.
Arguments:
- generated: float32 [8192, 1024], P(('grp', 'dev')), may hold values from -16 to 16
- data: float32 [8192, 1024], P(('grp', 'dev')), may hold values from -24 to 24
Outputs:
- force_rows: float32 [8192, 1024], P(('grp', 'dev'))
- energy: float32 [], replicated
The draws below stay inside these ranges and needn't reach their ends.
All inputs are finite; a program needn't handle non-finite values.
Results may differ from the reference program's by a relative error of at most 0.0002.
Values sent between devices are 32-bit elements; how exact they have to be, the bound alone decides.
No kernel may reach another device: no remote copies, remote signals or barrier semaphores. Data moves between devices by JAX's collectives and lax.ppermute only.
A program may use at most 64 MiB of HBM per device.

```python
import math
import jax
import jax.numpy as jnp
from jax import lax

D = 1024
GEN_DEV = 16
DATA_DEV = 16
GEN_ALL = 8192
DATA_ALL = 8192
N_DEV = 32


def cluster_base(key_centers, key_first, key_second, key_weights, count, width):
    centers = jnp.clip(0.7 * jax.random.normal(key_centers, (16, width), jnp.float32), -2.0, 2.0)
    first = jax.random.randint(key_first, (count,), 0, 16)
    second = jax.random.randint(key_second, (count,), 0, 16)
    weights = jax.random.uniform(key_weights, (count, 2), jnp.float32, 0.3, 1.0)
    return weights[:, 0:1] * centers[first] + weights[:, 1:2] * centers[second]


def draw_generated(key, part):
    key = jax.random.fold_in(key, 11)
    keys = jax.random.split(key, 7)
    base = cluster_base(keys[0], keys[1], keys[2], keys[3], GEN_ALL, D)
    coord = jnp.exp(jax.random.uniform(keys[4], (1, D), jnp.float32, math.log(0.4), math.log(1.2)))
    scales = jnp.exp(jax.random.uniform(keys[5], (GEN_ALL, 1), jnp.float32, math.log(0.3), math.log(1.8)))
    noise = jnp.clip(jax.random.normal(keys[6], (GEN_ALL, D), jnp.float32), -3.0, 3.0) * coord
    return scales * (base + noise)


def draw_data(key, part):
    key = jax.random.fold_in(key, 23)
    keys = jax.random.split(key, 7)
    base = cluster_base(keys[0], keys[1], keys[2], keys[3], DATA_ALL, D)
    coord = jnp.exp(jax.random.uniform(keys[4], (1, D), jnp.float32, math.log(0.4), math.log(1.2)))
    scales = jnp.exp(jax.random.uniform(keys[5], (DATA_ALL, 1), jnp.float32, math.log(0.4), math.log(2.6)))
    noise = jnp.clip(jax.random.normal(keys[6], (DATA_ALL, D), jnp.float32), -3.0, 3.0) * coord
    return scales * (base + noise)


def setup_inputs(seed: int = 0) -> dict:
    arg_keys = jax.random.split(jax.random.key(seed), 3)
    return {
        "generated": draw_generated(jax.random.fold_in(arg_keys[2], 71), 0),
        "data": draw_data(jax.random.fold_in(arg_keys[2], 71), 0),
    }


HIGH = lax.Precision.HIGHEST

def distances(left, right):
    left_sq = lax.optimization_barrier(jnp.sum(left * left, axis=1))
    right_sq = lax.optimization_barrier(jnp.sum(right * right, axis=1))
    inner = lax.dot_general(left, right, (((1,), (1,)), ((), ())), precision=HIGH, preferred_element_type=jnp.float32)
    return jnp.sqrt(jnp.maximum(left_sq[:, None] + right_sq[None, :] - 2.0 * inner, 0.0) + 1.0)

def reference(generated, data):
    n_gen = GEN_ALL
    n_data = DATA_ALL
    root_width = D ** 0.5

    def gen_part(row_block):
        to_gen = distances(row_block, generated)
        to_data = distances(row_block, data)
        energy_part = -jnp.sum(to_gen) / (n_gen * n_gen) + jnp.sum(to_data) / (n_gen * n_data)
        weight_gen = -root_width / n_gen / to_gen
        weight_data = root_width / n_data / to_data
        totals = lax.optimization_barrier(jnp.sum(weight_gen, axis=1)) + lax.optimization_barrier(jnp.sum(weight_data, axis=1))
        force_block = totals[:, None] * row_block
        force_block = force_block - jnp.dot(weight_gen, generated, precision=HIGH, preferred_element_type=jnp.float32)
        force_block = force_block - jnp.dot(weight_data, data, precision=HIGH, preferred_element_type=jnp.float32)
        return (energy_part, force_block)

    def data_part(row_block):
        to_gen = distances(row_block, generated)
        to_data = distances(row_block, data)
        return jnp.sum(to_gen) / (n_gen * n_data) - jnp.sum(to_data) / (n_data * n_data)
    gen_energies, forces = lax.map(gen_part, generated.reshape(-1, GEN_DEV * N_DEV, D))
    data_energies = lax.map(data_part, data.reshape(-1, DATA_DEV * N_DEV, D))
    energy = (jnp.sum(gen_energies) + jnp.sum(data_energies)) / root_width
    return (forces.reshape(GEN_ALL, D), energy)
```

```python
import jax
import jax.numpy as jnp
from jax import lax
from jax.experimental import pallas as pl
from jax.experimental.pallas import tpu as pltpu
from jax.sharding import Mesh, PartitionSpec as P

AXES = ("x", "yh", "z", "yl", "c")
SIZES = (4, 4, 8, 2, 2)
ROOT_WIDTH = 32.0
COUNT = 8192.0
NT = (((1,), (1,)), ((), ()))
NN = (((1,), (0,)), ((), ()))


def halves(value):
    high = value.astype(jnp.bfloat16)
    low = (value - high.astype(jnp.float32)).astype(jnp.bfloat16)
    return high, low


def product(left, right, dims):
    def dot(a, b):
        return lax.dot_general(a, b, dims, preferred_element_type=jnp.float32)

    return dot(left[0], right[0]) + (dot(left[0], right[1]) + dot(left[1], right[0]))


def flat(block):
    return block.reshape(block.shape[0] * block.shape[1], block.shape[2])


def pair_kernel(rows_ref, cols_ref, force_ref, energy_ref):
    own = rows_ref.shape[1] // 2
    row_gen = flat(rows_ref[:, :own, :])
    row_data = flat(rows_ref[:, own:, :])
    count = row_gen.shape[0]
    rows = jnp.concatenate([row_gen, row_data], axis=0)
    rows_sq = jnp.sum(rows * rows, axis=1, keepdims=True)
    rows_hl = halves(rows)
    chunk = 16
    total = jnp.zeros((count, 1), jnp.float32)
    force = jnp.zeros(row_gen.shape, jnp.float32)
    energy = jnp.zeros((1, chunk * own), jnp.float32)
    for kind in range(2):
        for start in range(0, cols_ref.shape[0], chunk):
            cols = flat(cols_ref[start : start + chunk, kind * own : (kind + 1) * own, :])
            cols_sq = jnp.sum(cols * cols, axis=1, keepdims=True)
            cols_sq = jnp.transpose(jnp.broadcast_to(cols_sq, (cols.shape[0], 128)))[0:1, :]
            cols_hl = halves(cols)
            used = count if kind == 0 else 2 * count
            inner = product((rows_hl[0][:used], rows_hl[1][:used]), cols_hl, NT)
            square = jnp.maximum(rows_sq[:used] + cols_sq - 2.0 * inner, 0.0) + 1.0
            inverse = lax.rsqrt(square)
            distance = square * inverse
            near = jnp.sum(distance[:count], axis=0, keepdims=True)
            if kind == 0:
                energy = energy - near
            else:
                energy = energy + 2.0 * near
                energy = energy - jnp.sum(distance[count:], axis=0, keepdims=True)
            coef = (-1.0 if kind == 0 else 1.0) * ROOT_WIDTH / COUNT
            weight = coef * inverse[:count]
            total = total + jnp.sum(weight, axis=1, keepdims=True)
            force = force + product(halves(weight), cols_hl, NN)
    force_ref[...] = total * row_gen - force
    energy_ref[...] = jnp.broadcast_to(
        jnp.sum(energy, axis=1, keepdims=True) / (COUNT * COUNT * ROOT_WIDTH), energy_ref.shape
    )


def pairs(rows, cols):
    count = rows.shape[0] * rows.shape[1] // 2
    width = rows.shape[2]
    return pl.pallas_call(
        pair_kernel,
        out_shape=(
            jax.ShapeDtypeStruct((count, width), jnp.float32),
            jax.ShapeDtypeStruct((8, 128), jnp.float32),
        ),
        in_specs=[pl.BlockSpec(memory_space=pltpu.VMEM)] * 2,
        out_specs=[pl.BlockSpec(memory_space=pltpu.VMEM)] * 2,
        compiler_params=pltpu.CompilerParams(vmem_limit_bytes=48 * 1024 * 1024),
        cost_estimate=pl.CostEstimate(flops=4_000_000_000, bytes_accessed=8_000_000, transcendentals=400_000),
    )(rows, cols)


def exchanged(value, axes):
    return lax.all_to_all(value, axes, split_axis=0, concat_axis=0, tiled=True)


def body(generated, data):
    own = jnp.concatenate([generated, data], axis=0)
    cols = lax.all_gather(own, ("x", "z"), axis=0, tiled=False)
    line = exchanged(jnp.broadcast_to(own[None], (8,) + own.shape), ("yh", "yl"))
    other = lax.ppermute(line, "c", [(0, 1), (1, 0)])
    core = lax.axis_index("c")
    first = jnp.where(core == 0, line, other)
    second = jnp.where(core == 0, other, line)
    rows = jnp.stack([first, second], axis=1).reshape(16, 32, 1024)
    force, energy = pairs(rows, cols)
    force = exchanged(force.reshape(16, 16, 1024), ("yh", "yl", "c"))
    force_rows = jnp.sum(force, axis=0)
    energy = jnp.sum(exchanged(jnp.broadcast_to(energy[None, :1], (16, 1, 128)), ("yh", "yl", "c")), axis=0)
    energy = jnp.sum(exchanged(jnp.broadcast_to(energy[None], (32, 1, 128)), ("x", "z")), axis=0)
    return (force_rows, energy[0, 0])


def solution(mesh):
    fine = Mesh(mesh.devices.reshape(SIZES), AXES)
    placed = P(AXES, None)
    return jax.shard_map(body, mesh=fine, in_specs=(placed, placed), out_specs=(placed, P()), check_vma=False)
```

```python
import jax
import jax.numpy as jnp
from jax import lax
from jax.experimental import pallas as pl
from jax.experimental.pallas import tpu as pltpu
from jax.sharding import Mesh, PartitionSpec as P

AXES = ("x", "yh", "z", "yl", "c")
SIZES = dict(zip(AXES, (4, 4, 8, 2, 2)))
Y = ("yh", "yl")
OWN = 16
WIDTH = 1024
ROOT_WIDTH = 32.0
COUNT = 8192.0
NT = (((1,), (1,)), ((), ()))
NN = (((1,), (0,)), ((), ()))


def halves(value):
    high = value.astype(jnp.bfloat16)
    low = (value - high.astype(jnp.float32)).astype(jnp.bfloat16)
    return high, low


def product(left, right, dims):
    def dot(a, b):
        return lax.dot_general(a, b, dims, preferred_element_type=jnp.float32)

    return dot(left[0], right[0]) + (dot(left[0], right[1]) + dot(left[1], right[0]))


def flat(block):
    return block.reshape(block.shape[0] * block.shape[1], block.shape[2])


def pair_kernel(n_cols, line_ref, other_ref, *refs):
    col_refs = refs[:n_cols]
    mine_ref, away_ref, energy_ref, high_ref, low_ref = refs[n_cols:]
    units = [ref[member] for ref in (line_ref, other_ref) for member in range(ref.shape[0])]
    half = len(units) // 2 * OWN
    row_gen = jnp.concatenate([unit[:OWN] for unit in units], axis=0)
    row_data = jnp.concatenate([unit[OWN:] for unit in units], axis=0)
    count = 2 * half
    rows = jnp.concatenate([row_gen, row_data], axis=0)
    rows_sq = jnp.sum(rows * rows, axis=1, keepdims=True)
    rows_hl = halves(rows)
    squares = []
    for kind in range(2):
        at = 0
        for ref in col_refs:
            cols = flat(ref[:, kind * OWN : (kind + 1) * OWN, :])
            squares.append(jnp.sum(cols * cols, axis=1, keepdims=True))
            high, low = halves(cols)
            high_ref[kind, at : at + cols.shape[0], :] = high
            low_ref[kind, at : at + cols.shape[0], :] = low
            at += cols.shape[0]
    depth = high_ref.shape[1]
    squares = jnp.concatenate(squares, axis=0)
    squares = jnp.transpose(jnp.broadcast_to(squares, (2 * depth, 128)))[0:1, :]
    chunk = 256
    total = jnp.zeros((count, 1), jnp.float32)
    force = jnp.zeros(row_gen.shape, jnp.float32)
    energy = jnp.zeros((1, chunk), jnp.float32)
    for kind in range(2):
        for start in range(0, depth, chunk):
            cols_hl = (high_ref[kind, start : start + chunk, :], low_ref[kind, start : start + chunk, :])
            cols_sq = squares[:, kind * depth + start : kind * depth + start + chunk]
            used = count if kind == 0 else 2 * count
            inner = product((rows_hl[0][:used], rows_hl[1][:used]), cols_hl, NT)
            square = jnp.maximum(rows_sq[:used] + cols_sq - 2.0 * inner, 0.0) + 1.0
            inverse = lax.rsqrt(square)
            distance = square * inverse
            near = jnp.sum(distance[:count], axis=0, keepdims=True)
            if kind == 0:
                energy = energy - near
            else:
                energy = energy + 2.0 * near
                energy = energy - jnp.sum(distance[count:], axis=0, keepdims=True)
            coef = (-1.0 if kind == 0 else 1.0) * ROOT_WIDTH / COUNT
            weight = coef * inverse[:count]
            total = total + jnp.sum(weight, axis=1, keepdims=True)
            force = force + product(halves(weight), cols_hl, NN)
    force = total * row_gen - force
    for member in range(len(units) // 2):
        mine_ref[member] = force[member * OWN : (member + 1) * OWN]
        away_ref[member] = force[half + member * OWN : half + (member + 1) * OWN]
    energy_ref[...] = jnp.broadcast_to(
        jnp.sum(energy, axis=1, keepdims=True) / (COUNT * COUNT * ROOT_WIDTH), energy_ref.shape
    )


def pairs(line, other, cols):
    members = line.shape[0]
    depth = sum(c.shape[0] for c in cols) * OWN
    vmem = pl.BlockSpec(memory_space=pltpu.VMEM)

    def kernel(*refs):
        pair_kernel(len(cols), *refs)

    return pl.pallas_call(
        kernel,
        out_shape=(
            jax.ShapeDtypeStruct((members, OWN, WIDTH), jnp.float32),
            jax.ShapeDtypeStruct((members, OWN, WIDTH), jnp.float32),
            jax.ShapeDtypeStruct((8, 128), jnp.float32),
        ),
        in_specs=[vmem] * (2 + len(cols)),
        out_specs=[vmem] * 3,
        scratch_shapes=[pltpu.VMEM((2, depth, WIDTH), jnp.bfloat16)] * 2,
        compiler_params=pltpu.CompilerParams(vmem_limit_bytes=40 * 1024 * 1024),
        cost_estimate=pl.CostEstimate(flops=4_000_000_000, bytes_accessed=8_000_000, transcendentals=400_000),
    )(line, other, *cols)


def sent(value, axes, move):
    sizes = [SIZES[a] for a in axes]
    perm = []
    total = 1
    for s in sizes:
        total *= s
    for source in range(total):
        rest, place = source, []
        for s in reversed(sizes):
            place.insert(0, rest % s)
            rest //= s
        target = 0
        for s, p in zip(sizes, move(*place)):
            target = target * s + p % s
        perm.append((source, target))
    return lax.ppermute(value, axes, perm)


def exchanged(value, axes):
    return lax.all_to_all(value, axes, split_axis=0, concat_axis=0, tiled=True)


def swapped(value):
    return sent(value, ("c",), lambda c: (1 - c,))


def shifted(value, axis, steps):
    return sent(value, (axis, "c"), lambda place, c: (place + steps * (1 - 2 * c), c))


def exchanged(value, axes):
    return lax.all_to_all(value, axes, split_axis=0, concat_axis=0, tiled=True)


def swapped(value):
    return sent(value, ("c",), lambda c: (1 - c,))


def joined(*parts):
    return jnp.concatenate(parts, axis=0)


def columns(own):
    parity = [own]
    for _ in range(3):
        parity.append(shifted(parity[-1], "z", 2))
    first = jnp.stack(parity)
    second = shifted(first, "x", 1)
    third = shifted(second, "x", 1)
    fourth = shifted(third, "x", 1)
    early, late = joined(first, second), joined(third, fourth)
    return [early, swapped(early), late, swapped(late)]


def body(generated, data):
    own = jnp.concatenate([generated, data], axis=0)
    line = exchanged(jnp.broadcast_to(own[None], (8,) + own.shape), Y)
    mine, away, energy = pairs(line, shifted(line, "z", -1), columns(own))
    energy = jnp.broadcast_to(energy[None, :1], (32, 1, 128))
    energy = jnp.sum(exchanged(energy, ("x", "z")), axis=0)
    mine = mine + shifted(away, "z", 1)
    force_rows = jnp.sum(exchanged(mine, Y), axis=0)
    energy = energy + swapped(energy)
    for bit in (1, 2, 4):
        energy = energy + sent(energy, Y, lambda hi, lo: divmod((2 * hi + lo) ^ bit, 2))
    return (force_rows, energy[0, 0])


def solution(mesh):
    fine = Mesh(mesh.devices.reshape(tuple(SIZES.values())), AXES)
    placed = P(AXES, None)
    return jax.shard_map(body, mesh=fine, in_specs=(placed, placed), out_specs=(placed, P()), check_vma=False)
```

```python
import jax
import jax.numpy as jnp
from jax import lax
from jax.experimental import pallas as pl
from jax.experimental.pallas import tpu as pltpu
from jax.sharding import Mesh, PartitionSpec as P

AXES = ("x", "yh", "zh", "zl", "yl", "c")
SIZES = dict(zip(AXES, (4, 4, 4, 2, 2, 2)))
Y = ("yh", "yl")
Z = ("zh", "zl")
STEPS = (0, 6, 2, 4)
OWN = 16
WIDTH = 1024
ROOT_WIDTH = 32.0
COUNT = 8192.0
NT = (((1,), (1,)), ((), ()))
NN = (((1,), (0,)), ((), ()))


def halves(value):
    high = value.astype(jnp.bfloat16)
    low = (value - high.astype(jnp.float32)).astype(jnp.bfloat16)
    return high, low


def product(left, right, dims):
    def dot(a, b):
        return lax.dot_general(a, b, dims, preferred_element_type=jnp.float32)

    return dot(left[0], right[0]) + (dot(left[0], right[1]) + dot(left[1], right[0]))


def flat(block):
    return block.reshape(block.shape[0] * block.shape[1], block.shape[2])


def pair_kernel(n_cols, place_ref, line_ref, other_ref, *refs):
    col_refs = refs[:n_cols]
    mine_ref, away_ref, energy_ref, high_ref, low_ref = refs[n_cols:]
    units = [ref[member] for ref in (line_ref, other_ref) for member in range(ref.shape[0])]
    half = len(units) // 2 * OWN
    row_gen = jnp.concatenate([unit[:OWN] for unit in units], axis=0)
    row_data = jnp.concatenate([unit[OWN:] for unit in units], axis=0)
    count = 2 * half
    rows = jnp.concatenate([row_gen, row_data], axis=0)
    rows_sq = jnp.sum(rows * rows, axis=1, keepdims=True)
    rows_hl = halves(rows)
    squares = []
    for kind in range(2):
        at = 0
        for ref in col_refs:
            cols = flat(ref[:, kind * OWN : (kind + 1) * OWN, :])
            squares.append(jnp.sum(cols * cols, axis=1, keepdims=True))
            high, low = halves(cols)
            high_ref[kind, at : at + cols.shape[0], :] = high
            low_ref[kind, at : at + cols.shape[0], :] = low
            at += cols.shape[0]
    depth = high_ref.shape[1]
    squares = jnp.concatenate(squares, axis=0)
    squares = jnp.transpose(jnp.broadcast_to(squares, (2 * depth, 128)))[0:1, :]
    chunk = 256
    total = jnp.zeros((count, 1), jnp.float32)
    force = jnp.zeros(row_gen.shape, jnp.float32)
    energy = jnp.zeros((1, chunk), jnp.float32)
    for kind in range(2):
        for start in range(0, depth, chunk):
            cols_hl = (high_ref[kind, start : start + chunk, :], low_ref[kind, start : start + chunk, :])
            cols_sq = squares[:, kind * depth + start : kind * depth + start + chunk]
            used = count if kind == 0 else 2 * count
            inner = product((rows_hl[0][:used], rows_hl[1][:used]), cols_hl, NT)
            square = jnp.maximum(rows_sq[:used] + cols_sq - 2.0 * inner, 0.0) + 1.0
            inverse = lax.rsqrt(square)
            distance = square * inverse
            near = jnp.sum(distance[:count], axis=0, keepdims=True)
            if kind == 0:
                energy = energy - near
            else:
                energy = energy + 2.0 * near
                energy = energy - jnp.sum(distance[count:], axis=0, keepdims=True)
            coef = (-1.0 if kind == 0 else 1.0) * ROOT_WIDTH / COUNT
            weight = coef * inverse[:count]
            total = total + jnp.sum(weight, axis=1, keepdims=True)
            force = force + product(halves(weight), cols_hl, NN)
    force = total * row_gen - force
    for member in range(len(units) // 2):
        to = lax.rem(place_ref[member // len(STEPS)] + STEPS[member % len(STEPS)], 8)
        mine_ref[to] = force[member * OWN : (member + 1) * OWN]
        away_ref[to] = force[half + member * OWN : half + (member + 1) * OWN]
    energy_ref[...] = jnp.broadcast_to(
        jnp.sum(energy, axis=1, keepdims=True) / (COUNT * COUNT * ROOT_WIDTH), energy_ref.shape
    )


def pairs(place, line, other, cols):
    members = line.shape[0]
    depth = sum(c.shape[0] for c in cols) * OWN
    vmem = pl.BlockSpec(memory_space=pltpu.VMEM)

    def kernel(*refs):
        pair_kernel(len(cols), *refs)

    return pl.pallas_call(
        kernel,
        out_shape=(
            jax.ShapeDtypeStruct((members, OWN, WIDTH), jnp.float32),
            jax.ShapeDtypeStruct((members, OWN, WIDTH), jnp.float32),
            jax.ShapeDtypeStruct((8, 128), jnp.float32),
        ),
        in_specs=[pl.BlockSpec(memory_space=pltpu.SMEM)] + [vmem] * (2 + len(cols)),
        out_specs=[vmem] * 3,
        scratch_shapes=[pltpu.VMEM((2, depth, WIDTH), jnp.bfloat16)] * 2,
        compiler_params=pltpu.CompilerParams(vmem_limit_bytes=24 * 1024 * 1024),
        cost_estimate=pl.CostEstimate(flops=4_000_000_000, bytes_accessed=8_000_000, transcendentals=400_000),
    )(place, line, other, *cols)


def sent(value, axes, move):
    sizes = [SIZES[a] for a in axes]
    perm = []
    total = 1
    for s in sizes:
        total *= s
    for source in range(total):
        rest, place = source, []
        for s in reversed(sizes):
            place.insert(0, rest % s)
            rest //= s
        target = 0
        for s, p in zip(sizes, move(*place)):
            target = target * s + p % s
        perm.append((source, target))
    return lax.ppermute(value, axes, perm)


def exchanged(value, axes):
    return lax.all_to_all(value, axes, split_axis=0, concat_axis=0, tiled=True)


def swapped(value):
    return sent(value, ("c",), lambda c: (1 - c,))


def along(value, axes, steps):
    return sent(value, axes, lambda high, low: divmod((2 * high + low + steps) % 8, 2))


def shifted(value, axes, steps):
    def move(high, low, c):
        return (*divmod((2 * high + low + steps * (1 - 2 * c)) % 8, 2), c)

    return sent(value, (*axes, "c"), move)


def joined(*parts):
    return jnp.concatenate(parts, axis=0)


def body(generated, data):
    own = jnp.concatenate([generated, data], axis=0)
    parity = exchanged(jnp.broadcast_to(own[None], (4,) + own.shape), ("zh",))
    up, down = along(own, Y, 2), along(own, Y, -2)
    parity, up, down = lax.optimization_barrier((parity, up, down))
    cols = exchanged(jnp.broadcast_to(parity[None], (4,) + parity.shape), ("x",))
    line = jnp.stack([own, up, down, along(up, Y, 2)])
    line = joined(line, shifted(line, Y, -1))
    near = shifted(line, Z, -1)
    cols, near = lax.optimization_barrier((cols.reshape((16,) + own.shape), near))
    core = lax.axis_index("c")
    y = 2 * lax.axis_index("yh") + lax.axis_index("yl")
    place = jnp.stack([y, y + 9 - 2 * core]).astype(jnp.int32)
    mine, away, energy = pairs(place, line, near, [cols, swapped(cols)])
    energy = jnp.broadcast_to(energy[None, :1], (32, 1, 128))
    energy = jnp.sum(exchanged(energy, ("x", "zh", "zl")), axis=0)
    mine = mine + shifted(away, Z, 1)
    loaded = jnp.concatenate([mine, jnp.broadcast_to(energy[None], (8, OWN, 128))], axis=2)
    loaded = exchanged(loaded, Y)
    force_rows = jnp.sum(loaded[:, :, :WIDTH], axis=0)
    energy = jnp.sum(loaded[:, :1, WIDTH:], axis=0)
    energy = energy + swapped(energy)
    return (force_rows, energy[0, 0])


def solution(mesh):
    fine = Mesh(mesh.devices.reshape(tuple(SIZES.values())), AXES)
    placed = P(AXES, None)
    return jax.shard_map(body, mesh=fine, in_specs=(placed, placed), out_specs=(placed, P()), check_vma=False)
```

```python
import jax
import jax.numpy as jnp
from jax import lax
from jax.experimental import pallas as pl
from jax.experimental.pallas import tpu as pltpu
from jax.sharding import Mesh, PartitionSpec as P

AXES = ("x", "yh", "zh", "zl", "yl", "c")
SIZES = dict(zip(AXES, (4, 4, 4, 2, 2, 2)))
Y = ("yh", "yl")
Z = ("zh", "zl")
OWN = 16
WIDTH = 1024
LINE = 8
UNITS = 16
COUNT = LINE * 2 * OWN
DEPTH = UNITS * OWN
ROOT_WIDTH = 32.0
TOTAL = 8192.0
NT = (((1,), (1,)), ((), ()))
NN = (((1,), (0,)), ((), ()))
SMEM = pl.BlockSpec(memory_space=pltpu.SMEM)
VMEM = pl.BlockSpec(memory_space=pltpu.VMEM)
ANY = pl.BlockSpec(memory_space=pl.ANY)
PARAMS = pltpu.CompilerParams(vmem_limit_bytes=28 * 1024 * 1024)


def shape(*dims, dtype=jnp.float32):
    return jax.ShapeDtypeStruct(dims, dtype)


def cost(flops):
    return pl.CostEstimate(flops=flops, bytes_accessed=4_000_000, transcendentals=200_000)


def halves(value):
    high = value.astype(jnp.bfloat16)
    low = (value - high.astype(jnp.float32)).astype(jnp.bfloat16)
    return high, low


def product(left, right, dims):
    def dot(a, b):
        return lax.dot_general(a, b, dims, preferred_element_type=jnp.float32)

    return dot(left[0], right[0]) + (dot(left[0], right[1]) + dot(left[1], right[0]))


def flat(block):
    return block.reshape(block.shape[0] * block.shape[1], block.shape[2])


def started(copies):
    for copy in copies:
        copy.start()
    return copies


def row_copies(line_ref, near_ref, rows_buf, sems, kinds):
    return started(
        [
            pltpu.make_async_copy(
                ref.at[:, kind * OWN : (kind + 1) * OWN, :], rows_buf.at[kind, side], sems.at[2 * kind + side]
            )
            for kind in kinds
            for side, ref in enumerate((line_ref, near_ref))
        ]
    )


def col_copies(cols_ref, cols_buf, sems):
    return started(
        [
            pltpu.make_async_copy(cols_ref.at[:, kind * OWN : (kind + 1) * OWN, :], cols_buf.at[kind], sems.at[4 + kind])
            for kind in range(2)
        ]
    )


def sign(kind):
    return -1.0 if kind == 0 else 1.0


def pair_terms(line_ref, near_ref, cols_ref, rows_buf, cols_buf, sems, use):
    row_wait = row_copies(line_ref, near_ref, rows_buf, sems, range(2))
    col_wait = col_copies(cols_ref, cols_buf, sems)
    for copy in row_wait:
        copy.wait()
    rows = jnp.concatenate([flat(rows_buf[kind, side]) for kind in range(2) for side in range(2)], axis=0)
    rows_sq = jnp.sum(rows * rows, axis=1, keepdims=True)
    rows_hl = halves(rows)
    total = jnp.zeros((COUNT, 1), jnp.float32)
    energy = jnp.zeros((1, DEPTH), jnp.float32)
    for kind in range(2):
        col_wait[kind].wait()
        cols = flat(cols_buf[kind])
        cols_sq = jnp.sum(cols * cols, axis=1, keepdims=True)
        cols_sq = jnp.transpose(jnp.broadcast_to(cols_sq, (DEPTH, 128)))[0:1, :]
        cols_hl = halves(cols)
        used = COUNT if kind == 0 else 2 * COUNT
        inner = product((rows_hl[0][:used], rows_hl[1][:used]), cols_hl, NT)
        square = jnp.maximum(rows_sq[:used] + cols_sq - 2.0 * inner, 0.0) + 1.0
        inverse = lax.rsqrt(square)
        distance = square * inverse
        near = jnp.sum(distance[:COUNT], axis=0, keepdims=True)
        if kind == 0:
            energy = energy - near
        else:
            energy = energy + (2.0 * near - jnp.sum(distance[COUNT:], axis=0, keepdims=True))
        weight = (sign(kind) * ROOT_WIDTH / TOTAL) * inverse[:COUNT]
        total = total + jnp.sum(weight, axis=1, keepdims=True)
        use(kind, cols_hl, halves(weight))
    energy = jnp.sum(energy, axis=1, keepdims=True) / (TOTAL * TOTAL * ROOT_WIDTH)
    return total, energy


PAIR_SCRATCH = [
    pltpu.VMEM((2, 2, LINE, OWN, WIDTH), jnp.float32),
    pltpu.VMEM((2, UNITS, OWN, WIDTH), jnp.float32),
    pltpu.SemaphoreType.DMA((6,)),
]


def first_kernel(line_ref, near_ref, cols_ref, force_ref, total_ref, energy_ref, rows_buf, cols_buf, sems):
    force = []

    def use(kind, cols_hl, weight_hl):
        force.append(product(weight_hl, cols_hl, NN))

    total, energy = pair_terms(line_ref, near_ref, cols_ref, rows_buf, cols_buf, sems, use)
    force_ref[...] = force[0] + force[1]
    total_ref[...] = jnp.broadcast_to(total, total_ref.shape)
    energy_ref[...] = jnp.broadcast_to(energy, energy_ref.shape)


def first_pairs(line, near, cols):
    return pl.pallas_call(
        first_kernel,
        out_shape=(shape(COUNT, WIDTH), shape(COUNT, 128), shape(8, 128)),
        in_specs=[ANY] * 3,
        out_specs=[VMEM] * 3,
        scratch_shapes=PAIR_SCRATCH,
        compiler_params=PARAMS,
        cost_estimate=cost(2_000_000_000),
    )(line, near, cols)


def second_kernel(
    line_ref, near_ref, cols_ref, total_in, energy_in, high_ref, low_ref, total_ref, energy_ref, rows_buf, cols_buf, sems
):
    def use(kind, cols_hl, weight_hl):
        high_ref[kind], low_ref[kind] = weight_hl

    total, energy = pair_terms(line_ref, near_ref, cols_ref, rows_buf, cols_buf, sems, use)
    total_ref[...] = total_in[...] + total
    energy_ref[...] = energy_in[...] + energy


def second_pairs(line, near, cols, total, energy):
    weights = shape(2, COUNT, DEPTH, dtype=jnp.bfloat16)
    return pl.pallas_call(
        second_kernel,
        out_shape=(weights, weights, shape(COUNT, 128), shape(8, 128)),
        in_specs=[ANY] * 3 + [VMEM] * 2,
        out_specs=[VMEM] * 4,
        scratch_shapes=PAIR_SCRATCH,
        compiler_params=PARAMS,
        cost_estimate=cost(1_200_000_000),
    )(line, near, cols, total, energy)


def force_kernel(
    place_ref, line_ref, near_ref, cols_ref, high_ref, low_ref, total_ref, force_ref, mine_ref, away_ref, rows_buf, cols_buf, sems
):
    row_wait = row_copies(line_ref, near_ref, rows_buf, sems, range(1))
    col_wait = col_copies(cols_ref, cols_buf, sems)
    force = force_ref[...]
    for kind in range(2):
        col_wait[kind].wait()
        force = force + product((high_ref[kind], low_ref[kind]), halves(flat(cols_buf[kind])), NN)
    for copy in row_wait:
        copy.wait()
    for side, out_ref in enumerate((mine_ref, away_ref)):
        for member in range(LINE):
            at = (side * LINE + member) * OWN
            to = 2 * (member % 4) + place_ref[member // 4]
            total = total_ref[at : at + OWN, 0:1]
            out_ref[to] = total * rows_buf[0, side, member] - force[at : at + OWN]


def forces(place, line, near, cols, high, low, total, force):
    return pl.pallas_call(
        force_kernel,
        out_shape=(shape(LINE, OWN, WIDTH), shape(LINE, OWN, WIDTH)),
        in_specs=[SMEM] + [ANY] * 3 + [VMEM] * 4,
        out_specs=[VMEM] * 2,
        scratch_shapes=PAIR_SCRATCH,
        compiler_params=PARAMS,
        cost_estimate=cost(800_000_000),
    )(place, line, near, cols, high, low, total, force)


def spread_kernel(gen_ref, data_ref, own_ref, copies_ref):
    own_ref[:OWN], own_ref[OWN:] = gen_ref[...], data_ref[...]
    for peer in range(4):
        copies_ref[peer, :OWN], copies_ref[peer, OWN:] = gen_ref[...], data_ref[...]


def spread(generated, data):
    return pl.pallas_call(
        spread_kernel,
        out_shape=(shape(2 * OWN, WIDTH), shape(4, 2 * OWN, WIDTH)),
        in_specs=[VMEM] * 2,
        out_specs=[VMEM] * 2,
    )(generated, data)


def sent(value, axes, move):
    sizes = [SIZES[a] for a in axes]
    perm = []
    total = 1
    for s in sizes:
        total *= s
    for source in range(total):
        rest, place = source, []
        for s in reversed(sizes):
            place.insert(0, rest % s)
            rest //= s
        target = 0
        for s, p in zip(sizes, move(*place)):
            target = target * s + p % s
        perm.append((source, target))
    return lax.ppermute(value, axes, perm)


def exchanged(value, axes):
    return lax.all_to_all(value, axes, split_axis=0, concat_axis=0, tiled=True)


def swapped(value):
    return sent(value, ("c",), lambda c: (1 - c,))


def along(value, axes, steps):
    return sent(value, axes, lambda high, low: divmod((2 * high + low + steps) % 8, 2))


def shifted(value, axes, steps):
    def move(high, low, c):
        return (*divmod((2 * high + low + steps * (1 - 2 * c)) % 8, 2), c)

    return sent(value, (*axes, "c"), move)


def joined(*parts):
    return jnp.concatenate(parts, axis=0)


def body(generated, data):
    own, copies = spread(generated, data)
    line = exchanged(copies, ("yh",))
    parity = jnp.stack([own] + [along(own, Z, steps) for steps in (2, -2, 4)])
    parity, _ = lax.optimization_barrier((parity, line))
    cols = exchanged(jnp.broadcast_to(parity[None], (4,) + parity.shape), ("x",))
    line = joined(line, shifted(line, Y, -1))
    near = shifted(line, Z, -1)
    cols, near = lax.optimization_barrier((cols.reshape((UNITS,) + own.shape), near))
    other = swapped(cols)
    force, total, energy = first_pairs(line, near, cols)
    high, low, total, energy = second_pairs(line, near, other, total, energy)
    yl = lax.axis_index("yl")
    place = jnp.stack([yl, 1 - yl]).astype(jnp.int32)
    mine, away = forces(place, line, near, other, high, low, total, force)
    energy = jnp.broadcast_to(energy[None, :1], (32, 1, 128))
    energy = jnp.sum(exchanged(energy, ("x", "zh", "zl")), axis=0)
    mine = mine + shifted(away, Z, 1)
    loaded = jnp.concatenate([mine, jnp.broadcast_to(energy[None], (8, OWN, 128))], axis=2)
    loaded = exchanged(loaded, Y)
    force_rows = jnp.sum(loaded[:, :, :WIDTH], axis=0)
    energy = jnp.sum(loaded[:, :1, WIDTH:], axis=0)
    energy = energy + swapped(energy)
    return (force_rows, energy[0, 0])


def solution(mesh):
    fine = Mesh(mesh.devices.reshape(tuple(SIZES.values())), AXES)
    placed = P(AXES, None)
    return jax.shard_map(body, mesh=fine, in_specs=(placed, placed), out_specs=(placed, P()), check_vma=False)
```

```python
import jax
import jax.numpy as jnp
from jax import lax
from jax.experimental import pallas as pl
from jax.experimental.pallas import tpu as pltpu
from jax.sharding import Mesh, PartitionSpec as P

AXES = ("x", "yh", "zh", "zl", "yl", "c")
SIZES = dict(zip(AXES, (4, 4, 4, 2, 2, 2)))
Y = ("yh", "yl")
Z = ("zh", "zl")
OWN = 16
WIDTH = 1024
LINE = 8
UNITS = 16
COUNT = LINE * 2 * OWN
DEPTH = UNITS * OWN
ROOT_WIDTH = 32.0
TOTAL = 8192.0
NT = (((1,), (1,)), ((), ()))
NN = (((1,), (0,)), ((), ()))
SMEM = pl.BlockSpec(memory_space=pltpu.SMEM)
VMEM = pl.BlockSpec(memory_space=pltpu.VMEM)
HBM = pl.BlockSpec(memory_space=pltpu.HBM)
STEPS = (0, 2, 6, 4)
PARAMS = pltpu.CompilerParams(vmem_limit_bytes=28 * 1024 * 1024)


def shape(*dims, dtype=jnp.float32):
    return jax.ShapeDtypeStruct(dims, dtype)


def cost(flops):
    return pl.CostEstimate(flops=flops, bytes_accessed=4_000_000, transcendentals=200_000)


def halves(value):
    high = value.astype(jnp.bfloat16)
    low = (value - high.astype(jnp.float32)).astype(jnp.bfloat16)
    return high, low


def product(left, right, dims):
    def dot(a, b):
        return lax.dot_general(a, b, dims, preferred_element_type=jnp.float32)

    return dot(left[0], right[0]) + (dot(left[0], right[1]) + dot(left[1], right[0]))


def flat(block):
    return block.reshape(block.shape[0] * block.shape[1], block.shape[2])


def sign(kind):
    return -1.0 if kind == 0 else 1.0


def pair_kernel(place_ref, line_ref, near_ref, cols_ref, other_ref, mine_ref, away_ref, energy_ref, rows_buf, cols_buf, sems):
    def by_kind(kind):
        return slice(kind * OWN, (kind + 1) * OWN)

    row_wait = [
        pltpu.make_async_copy(ref.at[:, by_kind(kind), :], rows_buf.at[kind, side], sems.at[2 * kind + side])
        for kind in range(2)
        for side, ref in enumerate((line_ref, near_ref))
    ]
    col_wait = [
        pltpu.make_async_copy(ref.at[:, by_kind(kind), :], cols_buf.at[kind, side], sems.at[4 + 2 * kind + side])
        for kind in range(2)
        for side, ref in enumerate((cols_ref, other_ref))
    ]
    for copy in row_wait + col_wait:
        copy.start()
    for copy in row_wait:
        copy.wait()
    row_gen = jnp.concatenate([flat(rows_buf[0, side]) for side in range(2)], axis=0)
    row_data = jnp.concatenate([flat(rows_buf[1, side]) for side in range(2)], axis=0)
    rows = jnp.concatenate([row_gen, row_data], axis=0)
    rows_sq = jnp.sum(rows * rows, axis=1, keepdims=True)
    rows_hl = halves(rows)
    total = jnp.zeros((COUNT, 1), jnp.float32)
    energy = jnp.zeros((1, DEPTH), jnp.float32)
    force = jnp.zeros((COUNT, WIDTH), jnp.float32)
    for kind in range(2):
        for side in range(2):
            col_wait[2 * kind + side].wait()
            cols = flat(cols_buf[kind, side])
            cols_sq = jnp.sum(cols * cols, axis=1, keepdims=True)
            cols_sq = jnp.transpose(jnp.broadcast_to(cols_sq, (DEPTH, 128)))[0:1, :]
            cols_hl = halves(cols)
            used = COUNT if kind == 0 else 2 * COUNT
            inner = product((rows_hl[0][:used], rows_hl[1][:used]), cols_hl, NT)
            square = jnp.maximum(rows_sq[:used] + cols_sq - 2.0 * inner, 0.0) + 1.0
            inverse = lax.rsqrt(square)
            distance = square * inverse
            near = jnp.sum(distance[:COUNT], axis=0, keepdims=True)
            if kind == 0:
                energy = energy - near
            else:
                energy = energy + (2.0 * near - jnp.sum(distance[COUNT:], axis=0, keepdims=True))
            weight = (sign(kind) * ROOT_WIDTH / TOTAL) * inverse[:COUNT]
            total = total + jnp.sum(weight, axis=1, keepdims=True)
            force = force + product(halves(weight), cols_hl, NN)
    force = total * row_gen - force
    for side, out_ref in enumerate((mine_ref, away_ref)):
        for member in range(LINE):
            at = (side * LINE + member) * OWN
            to = lax.rem(place_ref[member // len(STEPS)] + STEPS[member % len(STEPS)], LINE)
            out_ref[to] = force[at : at + OWN]
    energy = jnp.sum(energy, axis=1, keepdims=True) / (TOTAL * TOTAL * ROOT_WIDTH)
    energy_ref[...] = jnp.broadcast_to(energy, energy_ref.shape)


def pairs(place, line, near, cols, other):
    return pl.pallas_call(
        pair_kernel,
        out_shape=(shape(LINE, OWN, WIDTH), shape(LINE, OWN, WIDTH), shape(8, 128)),
        in_specs=[SMEM] + [HBM] * 4,
        out_specs=[VMEM] * 3,
        scratch_shapes=[
            pltpu.VMEM((2, 2, LINE, OWN, WIDTH), jnp.float32),
            pltpu.VMEM((2, 2, UNITS, OWN, WIDTH), jnp.float32),
            pltpu.SemaphoreType.DMA((8,)),
        ],
        compiler_params=PARAMS,
        cost_estimate=cost(4_000_000_000),
    )(place, line, near, cols, other)


def sent(value, axes, move):
    sizes = [SIZES[a] for a in axes]
    perm = []
    total = 1
    for s in sizes:
        total *= s
    for source in range(total):
        rest, place = source, []
        for s in reversed(sizes):
            place.insert(0, rest % s)
            rest //= s
        target = 0
        for s, p in zip(sizes, move(*place)):
            target = target * s + p % s
        perm.append((source, target))
    return lax.ppermute(value, axes, perm)


def exchanged(value, axes):
    return lax.all_to_all(value, axes, split_axis=0, concat_axis=0, tiled=True)


def swapped(value):
    return sent(value, ("c",), lambda c: (1 - c,))


def along(value, axes, steps):
    return sent(value, axes, lambda high, low: divmod((2 * high + low + steps) % 8, 2))


def shifted(value, axes, steps):
    def move(high, low, c):
        return (*divmod((2 * high + low + steps * (1 - 2 * c)) % 8, 2), c)

    return sent(value, (*axes, "c"), move)


def joined(*parts):
    return jnp.concatenate(parts, axis=0)


def body(generated, data):
    own = joined(generated, data)
    parity = jnp.stack([own] + [along(own, Z, steps) for steps in (2, -2, 4)])
    line = jnp.stack([own] + [along(own, Y, -steps) for steps in STEPS[1:]])
    cols = exchanged(jnp.broadcast_to(parity[None], (4,) + parity.shape), ("x",))
    line = joined(line, shifted(line, Y, -1))
    near = shifted(line, Z, -1)
    cols, near = lax.optimization_barrier((cols.reshape((UNITS,) + own.shape), near))
    y = 2 * lax.axis_index("yh") + lax.axis_index("yl")
    place = jnp.stack([y, y + 9 - 2 * lax.axis_index("c")]).astype(jnp.int32)
    mine, away, energy = pairs(place, line, near, cols, swapped(cols))
    energy = jnp.broadcast_to(energy[None, :1], (32, 1, 128))
    energy = jnp.sum(exchanged(energy, ("x", "zh", "zl")), axis=0)
    mine = mine + shifted(away, Z, 1)
    loaded = jnp.concatenate([mine, jnp.broadcast_to(energy[None], (8, OWN, 128))], axis=2)
    loaded = exchanged(loaded, Y)
    force_rows = jnp.sum(loaded[:, :, :WIDTH], axis=0)
    energy = jnp.sum(loaded[:, :1, WIDTH:], axis=0)
    energy = energy + swapped(energy)
    return (force_rows, energy[0, 0])


def solution(mesh):
    fine = Mesh(mesh.devices.reshape(tuple(SIZES.values())), AXES)
    placed = P(AXES, None)
    return jax.shard_map(body, mesh=fine, in_specs=(placed, placed), out_specs=(placed, P()), check_vma=False)
```

```python
import jax
import jax.numpy as jnp
from jax import lax
from jax.experimental import pallas as pl
from jax.experimental.pallas import tpu as pltpu
from jax.sharding import Mesh, PartitionSpec as P

AXES = ("x", "yh", "zh", "zl", "yl", "c")
SIZES = dict(zip(AXES, (4, 4, 4, 2, 2, 2)))
Y = ("yh", "yl")
Z = ("zh", "zl")
OWN = 16
WIDTH = 1024
LINE = 8
UNITS = 16
COUNT = LINE * 4 * OWN
DEPTH = UNITS * OWN
ROOT_WIDTH = 32.0
TOTAL = 8192.0
NT = (((1,), (1,)), ((), ()))
NN = (((1,), (0,)), ((), ()))
SMEM = pl.BlockSpec(memory_space=pltpu.SMEM)
VMEM = pl.BlockSpec(memory_space=pltpu.VMEM)
PARAMS = pltpu.CompilerParams(vmem_limit_bytes=28 * 1024 * 1024)


def shape(*dims, dtype=jnp.float32):
    return jax.ShapeDtypeStruct(dims, dtype)


def cost(flops):
    return pl.CostEstimate(flops=flops, bytes_accessed=4_000_000, transcendentals=200_000)


def halves(value):
    high = value.astype(jnp.bfloat16)
    low = (value - high.astype(jnp.float32)).astype(jnp.bfloat16)
    return high, low


def product(left, right, dims):
    def dot(a, b):
        return lax.dot_general(a, b, dims, preferred_element_type=jnp.float32)

    return dot(left[0], right[0]) + (dot(left[0], right[1]) + dot(left[1], right[0]))


def flat(block):
    return block.reshape(block.shape[0] * block.shape[1], block.shape[2])


def sign(kind):
    return -1.0 if kind == 0 else 1.0


def pair_kernel(place_ref, *refs):
    row_refs, (cols_ref, mine_ref, away_ref, back_ref, energy_ref) = refs[:4], refs[4:]

    def rows_of(kind):
        return jnp.concatenate([flat(ref[:, kind * OWN : (kind + 1) * OWN, :]) for ref in row_refs], axis=0)

    row_gen = rows_of(0)
    rows = jnp.concatenate([row_gen, rows_of(1)], axis=0)
    rows_sq = jnp.sum(rows * rows, axis=1, keepdims=True)
    rows_hl = halves(rows)
    total = jnp.zeros((COUNT, 1), jnp.float32)
    energy = jnp.zeros((1, DEPTH), jnp.float32)
    force = jnp.zeros((COUNT, WIDTH), jnp.float32)
    for kind in range(2):
        cols = flat(cols_ref[:, kind * OWN : (kind + 1) * OWN, :])
        cols_sq = jnp.sum(cols * cols, axis=1, keepdims=True)
        cols_sq = jnp.transpose(jnp.broadcast_to(cols_sq, (DEPTH, 128)))[0:1, :]
        cols_hl = halves(cols)
        used = COUNT if kind == 0 else 2 * COUNT
        inner = product((rows_hl[0][:used], rows_hl[1][:used]), cols_hl, NT)
        square = jnp.maximum(rows_sq[:used] + cols_sq - 2.0 * inner, 0.0) + 1.0
        inverse = lax.rsqrt(square)
        distance = square * inverse
        near = jnp.sum(distance[:COUNT], axis=0, keepdims=True)
        if kind == 0:
            energy = energy - near
        else:
            energy = energy + (2.0 * near - jnp.sum(distance[COUNT:], axis=0, keepdims=True))
        weight = (sign(kind) * ROOT_WIDTH / TOTAL) * inverse[:COUNT]
        total = total + jnp.sum(weight, axis=1, keepdims=True)
        force = force + product(halves(weight), cols_hl, NN)
    force = total * row_gen - force
    outs = (mine_ref, away_ref, back_ref.at[0], back_ref.at[1])
    for group, out_ref in enumerate(outs):
        for member in range(LINE):
            at = (group * LINE + member) * OWN
            to = 2 * (member % 4) + place_ref[member // 4]
            out_ref[to] = force[at : at + OWN]
    energy = jnp.sum(energy, axis=1, keepdims=True) / (TOTAL * TOTAL * ROOT_WIDTH)
    energy_ref[...] = jnp.broadcast_to(energy, energy_ref.shape)


def pairs(place, rows, cols):
    part = shape(LINE, OWN, WIDTH)
    return pl.pallas_call(
        pair_kernel,
        out_shape=(part, part, shape(2, LINE, OWN, WIDTH), shape(8, 128)),
        in_specs=[SMEM] + [VMEM] * 5,
        out_specs=[VMEM] * 4,
        compiler_params=PARAMS,
        cost_estimate=cost(4_000_000_000),
    )(place, *rows, cols)


def spread_kernel(gen_ref, data_ref, own_ref, copies_ref):
    own_ref[:OWN], own_ref[OWN:] = gen_ref[...], data_ref[...]
    for peer in range(4):
        copies_ref[peer, :OWN], copies_ref[peer, OWN:] = gen_ref[...], data_ref[...]


def spread(generated, data):
    return pl.pallas_call(
        spread_kernel,
        out_shape=(shape(2 * OWN, WIDTH), shape(4, 2 * OWN, WIDTH)),
        in_specs=[VMEM] * 2,
        out_specs=[VMEM] * 2,
    )(generated, data)


def sent(value, axes, move):
    sizes = [SIZES[a] for a in axes]
    perm = []
    total = 1
    for s in sizes:
        total *= s
    for source in range(total):
        rest, place = source, []
        for s in reversed(sizes):
            place.insert(0, rest % s)
            rest //= s
        target = 0
        for s, p in zip(sizes, move(*place)):
            target = target * s + p % s
        perm.append((source, target))
    return lax.ppermute(value, axes, perm)


def exchanged(value, axes):
    return lax.all_to_all(value, axes, split_axis=0, concat_axis=0, tiled=True)


def swapped(value):
    return sent(value, ("c",), lambda c: (1 - c,))


def along(value, axes, steps):
    return sent(value, axes, lambda high, low: divmod((2 * high + low + steps) % 8, 2))


def shifted(value, axes, steps):
    def move(high, low, c):
        return (*divmod((2 * high + low + steps * (1 - 2 * c)) % 8, 2), c)

    return sent(value, (*axes, "c"), move)


def joined(*parts):
    return jnp.concatenate(parts, axis=0)


def body(generated, data):
    own, copies = spread(generated, data)
    line = exchanged(copies, ("yh",))
    parity = jnp.stack([own] + [along(own, Z, steps) for steps in (2, -2, 4)])
    parity, _ = lax.optimization_barrier((parity, line))
    cols = exchanged(jnp.broadcast_to(parity[None], (4,) + parity.shape), ("x",))
    line = joined(line, shifted(line, Y, -1))
    near = shifted(line, Z, -1)
    line_away = swapped(line)
    cols, near = lax.optimization_barrier((cols.reshape((UNITS,) + own.shape), near))
    yl = lax.axis_index("yl")
    place = jnp.stack([yl, 1 - yl]).astype(jnp.int32)
    mine, away, back, energy = pairs(place, (line, near, line_away, swapped(near)), cols)
    energy = jnp.broadcast_to(energy[None, :1], (64, 1, 128))
    energy = jnp.sum(exchanged(energy, ("x", "zh", "zl", "c")), axis=0)
    back = swapped(back)
    mine = mine + back[0] + shifted(away + back[1], Z, 1)
    loaded = jnp.concatenate([mine, jnp.broadcast_to(energy[None], (LINE, OWN, 128))], axis=2)
    loaded = exchanged(loaded, Y)
    force_rows = jnp.sum(loaded[:, :, :WIDTH], axis=0)
    energy = jnp.sum(loaded[:, 0, WIDTH:], axis=0)
    return (force_rows, energy[0])


def solution(mesh):
    fine = Mesh(mesh.devices.reshape(tuple(SIZES.values())), AXES)
    placed = P(AXES, None)
    return jax.shard_map(body, mesh=fine, in_specs=(placed, placed), out_specs=(placed, P()), check_vma=False)
```

```python
import jax
import jax.numpy as jnp
from jax import lax
from jax.experimental import pallas as pl
from jax.experimental.pallas import tpu as pltpu
from jax.sharding import Mesh, PartitionSpec as P

AXES = ("x", "yh", "zh", "zl", "yl", "c")
SIZES = dict(zip(AXES, (4, 4, 4, 2, 2, 2)))
Y = ("yh", "yl")
Z = ("zh", "zl")
OWN = 16
WIDTH = 1024
LINE = 8
UNITS = 16
COUNT = LINE * 4 * OWN
DEPTH = UNITS * OWN
ROOT_WIDTH = 32.0
TOTAL = 8192.0
NT = (((1,), (1,)), ((), ()))
NN = (((1,), (0,)), ((), ()))
SMEM = pl.BlockSpec(memory_space=pltpu.SMEM)
VMEM = pl.BlockSpec(memory_space=pltpu.VMEM)
PARAMS = pltpu.CompilerParams(vmem_limit_bytes=28 * 1024 * 1024)


def shape(*dims, dtype=jnp.float32):
    return jax.ShapeDtypeStruct(dims, dtype)


def cost(flops):
    return pl.CostEstimate(flops=flops, bytes_accessed=4_000_000, transcendentals=200_000)


def halves(value):
    high = value.astype(jnp.bfloat16)
    low = (value - high.astype(jnp.float32)).astype(jnp.bfloat16)
    return high, low


def product(left, right, dims):
    def dot(a, b):
        return lax.dot_general(a, b, dims, preferred_element_type=jnp.float32)

    return dot(left[0], right[0]) + (dot(left[0], right[1]) + dot(left[1], right[0]))


def flat(block):
    return block.reshape(block.shape[0] * block.shape[1], block.shape[2])


def sign(kind):
    return -1.0 if kind == 0 else 1.0


def pair_kernel(place_ref, *refs):
    row_refs, (cols_ref, mine_ref, away_ref, back_ref, energy_ref) = refs[:4], refs[4:]

    def rows_of(kind):
        return jnp.concatenate([flat(ref[:, kind * OWN : (kind + 1) * OWN, :]) for ref in row_refs], axis=0)

    row_gen = rows_of(0)
    rows = jnp.concatenate([row_gen, rows_of(1)], axis=0)
    rows_sq = jnp.sum(rows * rows, axis=1, keepdims=True)
    rows_hl = halves(rows)
    total = jnp.zeros((COUNT, 1), jnp.float32)
    energy = jnp.zeros((1, DEPTH), jnp.float32)
    force = jnp.zeros((COUNT, WIDTH), jnp.float32)
    for kind in range(2):
        cols = flat(cols_ref[:, kind * OWN : (kind + 1) * OWN, :])
        cols_sq = jnp.sum(cols * cols, axis=1, keepdims=True)
        cols_sq = jnp.transpose(jnp.broadcast_to(cols_sq, (DEPTH, 128)))[0:1, :]
        cols_hl = halves(cols)
        used = COUNT if kind == 0 else 2 * COUNT
        inner = product((rows_hl[0][:used], rows_hl[1][:used]), cols_hl, NT)
        square = jnp.maximum(rows_sq[:used] + cols_sq - 2.0 * inner, 0.0) + 1.0
        inverse = lax.rsqrt(square)
        distance = square * inverse
        near = jnp.sum(distance[:COUNT], axis=0, keepdims=True)
        if kind == 0:
            energy = energy - near
        else:
            energy = energy + (2.0 * near - jnp.sum(distance[COUNT:], axis=0, keepdims=True))
        weight = (sign(kind) * ROOT_WIDTH / TOTAL) * inverse[:COUNT]
        total = total + jnp.sum(weight, axis=1, keepdims=True)
        force = force + product(halves(weight), cols_hl, NN)
    force = total * row_gen - force
    outs = (mine_ref, away_ref, back_ref.at[0], back_ref.at[1])
    for group, out_ref in enumerate(outs):
        for member in range(LINE):
            at = (group * LINE + member) * OWN
            to = 2 * (member % 4) + place_ref[member // 4]
            out_ref[to, :, :WIDTH] = force[at : at + OWN]
    energy = jnp.sum(energy, axis=1, keepdims=True) / (TOTAL * TOTAL * ROOT_WIDTH)
    energy_ref[...] = jnp.broadcast_to(energy, energy_ref.shape)
    back_ref[:, :, :, WIDTH:] = jnp.broadcast_to(energy, (*back_ref.shape[:3], 128))


def pairs(place, rows, cols):
    part = shape(LINE, OWN, WIDTH)
    return pl.pallas_call(
        pair_kernel,
        out_shape=(part, part, shape(2, LINE, OWN, WIDTH + 128), shape(8, 128)),
        in_specs=[SMEM] + [VMEM] * 5,
        out_specs=[VMEM] * 4,
        compiler_params=PARAMS,
        cost_estimate=cost(4_000_000_000),
    )(place, *rows, cols)


def spread_kernel(gen_ref, data_ref, own_ref, copies_ref):
    own_ref[:OWN], own_ref[OWN:] = gen_ref[...], data_ref[...]
    for peer in range(4):
        copies_ref[peer, :OWN], copies_ref[peer, OWN:] = gen_ref[...], data_ref[...]


def spread(generated, data):
    return pl.pallas_call(
        spread_kernel,
        out_shape=(shape(2 * OWN, WIDTH), shape(4, 2 * OWN, WIDTH)),
        in_specs=[VMEM] * 2,
        out_specs=[VMEM] * 2,
    )(generated, data)


def sent(value, axes, move):
    sizes = [SIZES[a] for a in axes]
    perm = []
    total = 1
    for s in sizes:
        total *= s
    for source in range(total):
        rest, place = source, []
        for s in reversed(sizes):
            place.insert(0, rest % s)
            rest //= s
        target = 0
        for s, p in zip(sizes, move(*place)):
            target = target * s + p % s
        perm.append((source, target))
    return lax.ppermute(value, axes, perm)


def exchanged(value, axes):
    return lax.all_to_all(value, axes, split_axis=0, concat_axis=0, tiled=True)


def swapped(value):
    return sent(value, ("c",), lambda c: (1 - c,))


def along(value, axes, steps):
    return sent(value, axes, lambda high, low: divmod((2 * high + low + steps) % 8, 2))


def shifted(value, axes, steps):
    def move(high, low, c):
        return (*divmod((2 * high + low + steps * (1 - 2 * c)) % 8, 2), c)

    return sent(value, (*axes, "c"), move)


def joined(*parts):
    return jnp.concatenate(parts, axis=0)


def body(generated, data):
    own, copies = spread(generated, data)
    line = exchanged(copies, ("yh",))
    parity = jnp.stack([own] + [along(own, Z, steps) for steps in (2, -2, 4)])
    parity, _ = lax.optimization_barrier((parity, line))
    cols = exchanged(jnp.broadcast_to(parity[None], (4,) + parity.shape), ("x",))
    line = joined(line, shifted(line, Y, -1))
    near = shifted(line, Z, -1)
    line_away = swapped(line)
    cols, near = lax.optimization_barrier((cols.reshape((UNITS,) + own.shape), near))
    yl = lax.axis_index("yl")
    place = jnp.stack([yl, 1 - yl]).astype(jnp.int32)
    mine, away, back, energy = pairs(place, (line, near, line_away, swapped(near)), cols)
    back = swapped(back)
    energy = energy[:1] + back[0, 0, :1, WIDTH:]
    back = back[:, :, :, :WIDTH]
    energy = jnp.sum(exchanged(jnp.broadcast_to(energy[None], (32, 1, 128)), ("x", "zh", "zl")), axis=0)
    mine = mine + back[0] + shifted(away + back[1], Z, 1)
    loaded = jnp.concatenate([mine, jnp.broadcast_to(energy[None], (LINE, OWN, 128))], axis=2)
    loaded = exchanged(loaded, Y)
    force_rows = jnp.sum(loaded[:, :, :WIDTH], axis=0)
    energy = jnp.sum(loaded[:, 0, WIDTH:], axis=0)
    return (force_rows, energy[0])


def solution(mesh):
    fine = Mesh(mesh.devices.reshape(tuple(SIZES.values())), AXES)
    placed = P(AXES, None)
    return jax.shard_map(body, mesh=fine, in_specs=(placed, placed), out_specs=(placed, P()), check_vma=False)
```

```python
import jax
import jax.numpy as jnp
from jax import lax
from jax.experimental import pallas as pl
from jax.experimental.pallas import tpu as pltpu
from jax.sharding import Mesh, PartitionSpec as P

AXES = ("x", "yh", "zh", "zl", "yl", "c")
SIZES = dict(zip(AXES, (4, 4, 4, 2, 2, 2)))
Y = ("yh", "yl")
Z = ("zh", "zl")
OWN = 16
WIDTH = 1024
LINE = 8
UNITS = 16
COUNT = LINE * 2 * OWN
DEPTH = UNITS * OWN
ROOT_WIDTH = 32.0
TOTAL = 8192.0
NT = (((1,), (1,)), ((), ()))
NN = (((1,), (0,)), ((), ()))
SMEM = pl.BlockSpec(memory_space=pltpu.SMEM)
VMEM = pl.BlockSpec(memory_space=pltpu.VMEM)
PARAMS = pltpu.CompilerParams(vmem_limit_bytes=28 * 1024 * 1024)


def shape(*dims, dtype=jnp.float32):
    return jax.ShapeDtypeStruct(dims, dtype)


def cost(flops):
    return pl.CostEstimate(flops=flops, bytes_accessed=4_000_000, transcendentals=200_000)


def halves(value):
    high = value.astype(jnp.bfloat16)
    low = (value - high.astype(jnp.float32)).astype(jnp.bfloat16)
    return high, low


def product(left, right, dims):
    def dot(a, b):
        return lax.dot_general(a, b, dims, preferred_element_type=jnp.float32)

    return dot(left[0], right[0]) + (dot(left[0], right[1]) + dot(left[1], right[0]))


def flat(block):
    return block.reshape(block.shape[0] * block.shape[1], block.shape[2])


def sign(kind):
    return -1.0 if kind == 0 else 1.0


def pair_kernel(place_ref, first_ref, second_ref, cols_ref, *refs):
    row_refs, (out_refs, energy_ref) = (first_ref, second_ref), refs[-2:]
    before = refs[0][0:1, 0:1] if len(refs) == 3 else 0.0

    def rows_of(kind):
        return jnp.concatenate([flat(ref[:, kind * OWN : (kind + 1) * OWN, :]) for ref in row_refs], axis=0)

    row_gen = rows_of(0)
    rows = jnp.concatenate([row_gen, rows_of(1)], axis=0)
    rows_sq = jnp.sum(rows * rows, axis=1, keepdims=True)
    rows_hl = halves(rows)
    total = jnp.zeros((COUNT, 1), jnp.float32)
    energy = jnp.zeros((1, DEPTH), jnp.float32)
    force = jnp.zeros((COUNT, WIDTH), jnp.float32)
    for kind in range(2):
        cols = flat(cols_ref[:, kind * OWN : (kind + 1) * OWN, :])
        cols_sq = jnp.sum(cols * cols, axis=1, keepdims=True)
        cols_sq = jnp.transpose(jnp.broadcast_to(cols_sq, (DEPTH, 128)))[0:1, :]
        cols_hl = halves(cols)
        used = COUNT if kind == 0 else 2 * COUNT
        inner = product((rows_hl[0][:used], rows_hl[1][:used]), cols_hl, NT)
        square = jnp.maximum(rows_sq[:used] + cols_sq - 2.0 * inner, 0.0) + 1.0
        inverse = lax.rsqrt(square)
        distance = square * inverse
        near = jnp.sum(distance[:COUNT], axis=0, keepdims=True)
        if kind == 0:
            energy = energy - near
        else:
            energy = energy + (2.0 * near - jnp.sum(distance[COUNT:], axis=0, keepdims=True))
        weight = (sign(kind) * ROOT_WIDTH / TOTAL) * inverse[:COUNT]
        total = total + jnp.sum(weight, axis=1, keepdims=True)
        force = force + product(halves(weight), cols_hl, NN)
    force = total * row_gen - force
    for group in range(2):
        for member in range(LINE):
            at = (group * LINE + member) * OWN
            to = 2 * (member % 4) + place_ref[member // 4]
            out_refs[group, to, :, :WIDTH] = force[at : at + OWN]
    energy = before + jnp.sum(energy, axis=1, keepdims=True) / (TOTAL * TOTAL * ROOT_WIDTH)
    energy_ref[...] = jnp.broadcast_to(energy, energy_ref.shape)
    if out_refs.shape[-1] > WIDTH:
        out_refs[:, :, :, WIDTH:] = jnp.broadcast_to(energy, (*out_refs.shape[:3], 128))


def pairs(place, first, second, cols, *before, flops):
    extra = 128 * len(before)
    return pl.pallas_call(
        pair_kernel,
        out_shape=(shape(2, LINE, OWN, WIDTH + extra), shape(8, 128)),
        in_specs=[SMEM] + [VMEM] * (3 + len(before)),
        out_specs=[VMEM] * 2,
        compiler_params=PARAMS,
        cost_estimate=cost(flops),
    )(place, first, second, cols, *before)


def spread_kernel(gen_ref, data_ref, own_ref, copies_ref):
    own_ref[:OWN], own_ref[OWN:] = gen_ref[...], data_ref[...]
    for peer in range(4):
        copies_ref[peer, :OWN], copies_ref[peer, OWN:] = gen_ref[...], data_ref[...]


def spread(generated, data):
    return pl.pallas_call(
        spread_kernel,
        out_shape=(shape(2 * OWN, WIDTH), shape(4, 2 * OWN, WIDTH)),
        in_specs=[VMEM] * 2,
        out_specs=[VMEM] * 2,
    )(generated, data)


def sent(value, axes, move):
    sizes = [SIZES[a] for a in axes]
    perm = []
    total = 1
    for s in sizes:
        total *= s
    for source in range(total):
        rest, place = source, []
        for s in reversed(sizes):
            place.insert(0, rest % s)
            rest //= s
        target = 0
        for s, p in zip(sizes, move(*place)):
            target = target * s + p % s
        perm.append((source, target))
    return lax.ppermute(value, axes, perm)


def exchanged(value, axes):
    return lax.all_to_all(value, axes, split_axis=0, concat_axis=0, tiled=True)


def swapped(value):
    return sent(value, ("c",), lambda c: (1 - c,))


def along(value, axes, steps):
    return sent(value, axes, lambda high, low: divmod((2 * high + low + steps) % 8, 2))


def shifted(value, axes, steps):
    def move(high, low, c):
        return (*divmod((2 * high + low + steps * (1 - 2 * c)) % 8, 2), c)

    return sent(value, (*axes, "c"), move)


def joined(*parts):
    return jnp.concatenate(parts, axis=0)


def body(generated, data):
    own, copies = spread(generated, data)
    line = exchanged(copies, ("yh",))
    up, down, far = (along(own, Z, steps) for steps in (2, -2, 4))
    line, up, down = lax.optimization_barrier((line, up, down))
    parity = jnp.stack([own, up, down, far])
    cols = exchanged(jnp.broadcast_to(parity[None], (4,) + parity.shape), ("x",))
    line = joined(line, shifted(line, Y, -1))
    near = shifted(line, Z, -1)
    line_away, near_away = swapped(line), swapped(near)
    cols = cols.reshape((UNITS,) + own.shape)
    yl = lax.axis_index("yl")
    place = jnp.stack([yl, 1 - yl]).astype(jnp.int32)
    mine, energy = pairs(place, line, near, cols, flops=6_000_000_000)
    back, energy = pairs(place, line_away, near_away, cols, energy, flops=2_000_000_000)
    back = swapped(back)
    energy = energy[:1] + back[0, 0, :1, WIDTH:]
    back = back[:, :, :, :WIDTH]
    mine, away = mine[0], mine[1]
    energy = jnp.sum(exchanged(jnp.broadcast_to(energy[None], (32, 1, 128)), ("x", "zh", "zl")), axis=0)
    mine = mine + back[0] + shifted(away + back[1], Z, 1)
    loaded = jnp.concatenate([mine, jnp.broadcast_to(energy[None], (LINE, OWN, 128))], axis=2)
    loaded = exchanged(loaded, Y)
    force_rows = jnp.sum(loaded[:, :, :WIDTH], axis=0)
    energy = jnp.sum(loaded[:, 0, WIDTH:], axis=0)
    return (force_rows, energy[0])


def solution(mesh):
    fine = Mesh(mesh.devices.reshape(tuple(SIZES.values())), AXES)
    placed = P(AXES, None)
    return jax.shard_map(body, mesh=fine, in_specs=(placed, placed), out_specs=(placed, P()), check_vma=False)
```

```python
import jax
import jax.numpy as jnp
from jax import lax
from jax.experimental import pallas as pl
from jax.experimental.pallas import tpu as pltpu
from jax.sharding import Mesh, PartitionSpec as P

AXES = ("x", "yh", "zh", "zl", "yl", "c")
SIZES = dict(zip(AXES, (4, 4, 4, 2, 2, 2)))
Y = ("yh", "yl")
Z = ("zh", "zl")
OWN = 16
WIDTH = 1024
LINE = 8
UNITS = 16
COUNT = LINE * 2 * OWN
DEPTH = UNITS * OWN
ROOT_WIDTH = 32.0
TOTAL = 8192.0
NT = (((1,), (1,)), ((), ()))
NN = (((1,), (0,)), ((), ()))
SMEM = pl.BlockSpec(memory_space=pltpu.SMEM)
VMEM = pl.BlockSpec(memory_space=pltpu.VMEM)
PARAMS = pltpu.CompilerParams(vmem_limit_bytes=28 * 1024 * 1024)


def shape(*dims, dtype=jnp.float32):
    return jax.ShapeDtypeStruct(dims, dtype)


def cost(flops):
    return pl.CostEstimate(flops=flops, bytes_accessed=4_000_000, transcendentals=200_000)


def halves(value):
    high = value.astype(jnp.bfloat16)
    low = (value - high.astype(jnp.float32)).astype(jnp.bfloat16)
    return high, low


def product(left, right, dims):
    def dot(a, b):
        return lax.dot_general(a, b, dims, preferred_element_type=jnp.float32)

    return dot(left[0], right[0]) + (dot(left[0], right[1]) + dot(left[1], right[0]))


def flat(block):
    return block.reshape(block.shape[0] * block.shape[1], block.shape[2])


def sign(kind):
    return -1.0 if kind == 0 else 1.0


def pair_kernel(place_ref, first_ref, second_ref, cols_ref, *refs):
    row_refs, (out_refs, energy_ref) = (first_ref, second_ref), refs[-2:]
    before = refs[0][0:1, 0:1] if len(refs) == 3 else 0.0

    def rows_of(kind):
        return jnp.concatenate([flat(ref[:, kind * OWN : (kind + 1) * OWN, :]) for ref in row_refs], axis=0)

    row_gen = rows_of(0)
    rows = jnp.concatenate([row_gen, rows_of(1)], axis=0)
    rows_sq = jnp.sum(rows * rows, axis=1, keepdims=True)
    rows_hl = halves(rows)
    total = jnp.zeros((COUNT, 1), jnp.float32)
    energy = jnp.zeros((1, DEPTH), jnp.float32)
    force = jnp.zeros((COUNT, WIDTH), jnp.float32)
    for kind in range(2):
        cols = flat(cols_ref[:, kind * OWN : (kind + 1) * OWN, :])
        cols_sq = jnp.sum(cols * cols, axis=1, keepdims=True)
        cols_sq = jnp.transpose(jnp.broadcast_to(cols_sq, (DEPTH, 128)))[0:1, :]
        cols_hl = halves(cols)
        used = COUNT if kind == 0 else 2 * COUNT
        inner = product((rows_hl[0][:used], rows_hl[1][:used]), cols_hl, NT)
        square = jnp.maximum(rows_sq[:used] + cols_sq - 2.0 * inner, 0.0) + 1.0
        inverse = lax.rsqrt(square)
        distance = square * inverse
        near = jnp.sum(distance[:COUNT], axis=0, keepdims=True)
        if kind == 0:
            energy = energy - near
        else:
            energy = energy + (2.0 * near - jnp.sum(distance[COUNT:], axis=0, keepdims=True))
        weight = (sign(kind) * ROOT_WIDTH / TOTAL) * inverse[:COUNT]
        total = total + jnp.sum(weight, axis=1, keepdims=True)
        force = force + product(halves(weight), cols_hl, NN)
    force = total * row_gen - force
    for group in range(2):
        for member in range(LINE):
            at = (group * LINE + member) * OWN
            to = 2 * (member % 4) + place_ref[member // 4]
            out_refs[group, to, :, :WIDTH] = force[at : at + OWN]
    energy = before + jnp.sum(energy, axis=1, keepdims=True) / (TOTAL * TOTAL * ROOT_WIDTH)
    energy_ref[...] = jnp.broadcast_to(energy, energy_ref.shape)
    if out_refs.shape[-1] > WIDTH:
        out_refs[:, :, :, WIDTH:] = jnp.broadcast_to(energy, (*out_refs.shape[:3], 128))


def pairs(place, first, second, cols, *before, flops):
    extra = 128 * len(before)
    return pl.pallas_call(
        pair_kernel,
        out_shape=(shape(2, LINE, OWN, WIDTH + extra), shape(8, 128)),
        in_specs=[SMEM] + [VMEM] * (3 + len(before)),
        out_specs=[VMEM] * 2,
        compiler_params=PARAMS,
        cost_estimate=cost(flops),
    )(place, first, second, cols, *before)


def spread_kernel(gen_ref, data_ref, own_ref, copies_ref):
    own_ref[:OWN], own_ref[OWN:] = gen_ref[...], data_ref[...]
    for peer in range(4):
        copies_ref[peer, :OWN], copies_ref[peer, OWN:] = gen_ref[...], data_ref[...]


def spread(generated, data):
    return pl.pallas_call(
        spread_kernel,
        out_shape=(shape(2 * OWN, WIDTH), shape(4, 2 * OWN, WIDTH)),
        in_specs=[VMEM] * 2,
        out_specs=[VMEM] * 2,
    )(generated, data)


def sent(value, axes, move):
    sizes = [SIZES[a] for a in axes]
    perm = []
    total = 1
    for s in sizes:
        total *= s
    for source in range(total):
        rest, place = source, []
        for s in reversed(sizes):
            place.insert(0, rest % s)
            rest //= s
        target = 0
        for s, p in zip(sizes, move(*place)):
            target = target * s + p % s
        perm.append((source, target))
    return lax.ppermute(value, axes, perm)


def exchanged(value, axes):
    return lax.all_to_all(value, axes, split_axis=0, concat_axis=0, tiled=True)


def swapped(value):
    return sent(value, ("c",), lambda c: (1 - c,))


def along(value, axes, steps):
    return sent(value, axes, lambda high, low: divmod((2 * high + low + steps) % 8, 2))


def shifted(value, axes, steps):
    def move(high, low, c):
        return (*divmod((2 * high + low + steps * (1 - 2 * c)) % 8, 2), c)

    return sent(value, (*axes, "c"), move)


def joined(*parts):
    return jnp.concatenate(parts, axis=0)


def body(generated, data):
    own, copies = spread(generated, data)
    line = exchanged(copies, ("yh",))
    parity = jnp.stack([own] + [along(own, Z, steps) for steps in (2, -2, 4)])
    parity, _ = lax.optimization_barrier((parity, line))
    cols = exchanged(jnp.broadcast_to(parity[None], (4,) + parity.shape), ("x",))
    line = joined(line, shifted(line, Y, -1))
    near = shifted(line, Z, -1)
    line_away = swapped(line)
    cols, near = lax.optimization_barrier((cols.reshape((UNITS,) + own.shape), near))
    near_away = swapped(near)
    yl = lax.axis_index("yl")
    place = jnp.stack([yl, 1 - yl]).astype(jnp.int32)
    mine, energy = pairs(place, line, near, cols, flops=6_000_000_000)
    back, energy = pairs(place, line_away, near_away, cols, energy, flops=2_000_000_000)
    back = swapped(back)
    energy = energy[:1] + back[0, 0, :1, WIDTH:]
    back = back[:, :, :, :WIDTH]
    mine, away = mine[0], mine[1]
    energy = jnp.sum(exchanged(jnp.broadcast_to(energy[None], (32, 1, 128)), ("x", "zh", "zl")), axis=0)
    mine = mine + back[0] + shifted(away + back[1], Z, 1)
    loaded = jnp.concatenate([mine, jnp.broadcast_to(energy[None], (LINE, OWN, 128))], axis=2)
    loaded = exchanged(loaded, Y)
    force_rows = jnp.sum(loaded[:, :, :WIDTH], axis=0)
    energy = jnp.sum(loaded[:, 0, WIDTH:], axis=0)
    return (force_rows, energy[0])


def solution(mesh):
    fine = Mesh(mesh.devices.reshape(tuple(SIZES.values())), AXES)
    placed = P(AXES, None)
    return jax.shard_map(body, mesh=fine, in_specs=(placed, placed), out_specs=(placed, P()), check_vma=False)
```

```python
import functools

import jax
import jax.numpy as jnp
from jax import lax
from jax.experimental import pallas as pl
from jax.experimental.pallas import tpu as pltpu
from jax.sharding import Mesh, PartitionSpec as P

AXES = ("x", "yh", "zh", "zl", "yl", "c")
SIZES = dict(zip(AXES, (4, 4, 4, 2, 2, 2)))
Y = ("yh", "yl")
Z = ("zh", "zl")
OWN = 16
WIDTH = 1024
LINE = 8
UNITS = 16
COUNT = LINE * 2 * OWN
DEPTH = UNITS * OWN
ROOT_WIDTH = 32.0
TOTAL = 8192.0
NT = (((1,), (1,)), ((), ()))
NN = (((1,), (0,)), ((), ()))
SMEM = pl.BlockSpec(memory_space=pltpu.SMEM)
VMEM = pl.BlockSpec(memory_space=pltpu.VMEM)
PARAMS = pltpu.CompilerParams(vmem_limit_bytes=28 * 1024 * 1024)


def shape(*dims, dtype=jnp.float32):
    return jax.ShapeDtypeStruct(dims, dtype)


def cost(flops):
    return pl.CostEstimate(flops=flops, bytes_accessed=4_000_000, transcendentals=200_000)


def halves(value):
    high = value.astype(jnp.bfloat16)
    low = (value - high.astype(jnp.float32)).astype(jnp.bfloat16)
    return high, low


def product(left, right, dims):
    def dot(a, b):
        return lax.dot_general(a, b, dims, preferred_element_type=jnp.float32)

    return dot(left[0], right[0]) + (dot(left[0], right[1]) + dot(left[1], right[0]))


def flat(block):
    return block.reshape(block.shape[0] * block.shape[1], block.shape[2])


def sign(kind):
    return -1.0 if kind == 0 else 1.0


def pair_kernel(final, place_ref, first_ref, second_ref, *refs):
    row_refs = (first_ref, second_ref)
    if final:
        high_ref, low_ref, squares_ref, before_ref, out_refs, energy_ref = refs
    else:
        cols_ref, out_refs, energy_ref, high_ref, low_ref, squares_ref = refs
        for kind in range(2):
            cols = flat(cols_ref[:, kind * OWN : (kind + 1) * OWN, :])
            high_ref[kind], low_ref[kind] = halves(cols)
            squares = jnp.broadcast_to(jnp.sum(cols * cols, axis=1, keepdims=True), (DEPTH, 128))
            squares_ref[kind] = jnp.transpose(squares)[0:8, :]

    def rows_of(kind):
        return jnp.concatenate([flat(ref[:, kind * OWN : (kind + 1) * OWN, :]) for ref in row_refs], axis=0)

    row_gen = rows_of(0)
    rows = jnp.concatenate([row_gen, rows_of(1)], axis=0)
    rows_sq = jnp.sum(rows * rows, axis=1, keepdims=True)
    rows_hl = halves(rows)
    total = jnp.zeros((COUNT, 1), jnp.float32)
    energy = jnp.zeros((1, DEPTH), jnp.float32)
    force = jnp.zeros((COUNT, WIDTH), jnp.float32)
    for kind in range(2):
        cols_hl = (high_ref[kind], low_ref[kind])
        cols_sq = squares_ref[kind, 0:1, :]
        used = COUNT if kind == 0 else 2 * COUNT
        inner = product((rows_hl[0][:used], rows_hl[1][:used]), cols_hl, NT)
        square = jnp.maximum(rows_sq[:used] + cols_sq - 2.0 * inner, 0.0) + 1.0
        inverse = lax.rsqrt(square)
        distance = square * inverse
        near = jnp.sum(distance[:COUNT], axis=0, keepdims=True)
        if kind == 0:
            energy = energy - near
        else:
            energy = energy + (2.0 * near - jnp.sum(distance[COUNT:], axis=0, keepdims=True))
        weight = (sign(kind) * ROOT_WIDTH / TOTAL) * inverse[:COUNT]
        total = total + jnp.sum(weight, axis=1, keepdims=True)
        force = force + product(halves(weight), cols_hl, NN)
    force = total * row_gen - force
    for group in range(2):
        for member in range(LINE):
            at = (group * LINE + member) * OWN
            to = 2 * (member % 4) + place_ref[member // 4]
            out_refs[group, to, :, :WIDTH] = force[at : at + OWN]
    energy = jnp.sum(energy, axis=1, keepdims=True) / (TOTAL * TOTAL * ROOT_WIDTH)
    if final:
        energy = before_ref[0:1, 0:1] + energy
    energy_ref[...] = jnp.broadcast_to(energy, energy_ref.shape)
    if final:
        out_refs[:, :, :, WIDTH:] = jnp.broadcast_to(energy, (*out_refs.shape[:3], 128))


def pairs(place, first, second, *operands, flops):
    final = len(operands) > 1
    split = shape(2, DEPTH, WIDTH, dtype=jnp.bfloat16)
    outs = (shape(2, LINE, OWN, WIDTH + 128 * final), shape(8, 128))
    if not final:
        outs += (split, split, shape(2, 8, DEPTH))
    return pl.pallas_call(
        functools.partial(pair_kernel, final),
        out_shape=outs,
        in_specs=[SMEM] + [VMEM] * (2 + len(operands)),
        out_specs=[VMEM] * len(outs),
        compiler_params=PARAMS,
        cost_estimate=cost(flops),
    )(place, first, second, *operands)


def spread_kernel(gen_ref, data_ref, own_ref, copies_ref):
    own_ref[:OWN], own_ref[OWN:] = gen_ref[...], data_ref[...]
    for peer in range(4):
        copies_ref[peer, :OWN], copies_ref[peer, OWN:] = gen_ref[...], data_ref[...]


def spread(generated, data):
    return pl.pallas_call(
        spread_kernel,
        out_shape=(shape(2 * OWN, WIDTH), shape(4, 2 * OWN, WIDTH)),
        in_specs=[VMEM] * 2,
        out_specs=[VMEM] * 2,
    )(generated, data)


def layout_kernel(*refs):
    for peer in range(4):
        for unit, ref in enumerate(refs[:4]):
            refs[4][peer, unit] = ref[...]


def layout(*units):
    return pl.pallas_call(
        layout_kernel,
        out_shape=shape(4, 4, 2 * OWN, WIDTH),
        in_specs=[VMEM] * 4,
        out_specs=VMEM,
    )(*units)


def sent(value, axes, move):
    sizes = [SIZES[a] for a in axes]
    perm = []
    total = 1
    for s in sizes:
        total *= s
    for source in range(total):
        rest, place = source, []
        for s in reversed(sizes):
            place.insert(0, rest % s)
            rest //= s
        target = 0
        for s, p in zip(sizes, move(*place)):
            target = target * s + p % s
        perm.append((source, target))
    return lax.ppermute(value, axes, perm)


def exchanged(value, axes):
    return lax.all_to_all(value, axes, split_axis=0, concat_axis=0, tiled=True)


def swapped(value):
    return sent(value, ("c",), lambda c: (1 - c,))


def along(value, axes, steps):
    return sent(value, axes, lambda high, low: divmod((2 * high + low + steps) % 8, 2))


def shifted(value, axes, steps):
    def move(high, low, c):
        return (*divmod((2 * high + low + steps * (1 - 2 * c)) % 8, 2), c)

    return sent(value, (*axes, "c"), move)


def joined(*parts):
    return jnp.concatenate(parts, axis=0)


def body(generated, data):
    own, copies = spread(generated, data)
    line = exchanged(copies, ("yh",))
    up, down, far = (along(own, Z, steps) for steps in (2, -2, 4))
    parity, _ = lax.optimization_barrier((layout(own, up, down, far), line))
    cols = exchanged(parity, ("x",))
    line = joined(line, shifted(line, Y, -1))
    near = shifted(line, Z, -1)
    line_away = swapped(line)
    cols, near = lax.optimization_barrier((cols.reshape((UNITS,) + own.shape), near))
    near_away = swapped(near)
    yl = lax.axis_index("yl")
    place = jnp.stack([yl, 1 - yl]).astype(jnp.int32)
    mine, energy, *split = pairs(place, line, near, cols, flops=6_000_000_000)
    back, energy = pairs(place, line_away, near_away, *split, energy, flops=2_000_000_000)
    back = swapped(back)
    energy = energy[:1] + back[0, 0, :1, WIDTH:]
    back = back[:, :, :, :WIDTH]
    mine, away = mine[0], mine[1]
    energy = jnp.sum(exchanged(jnp.broadcast_to(energy[None], (32, 1, 128)), ("x", "zh", "zl")), axis=0)
    mine = mine + back[0] + shifted(away + back[1], Z, 1)
    loaded = jnp.concatenate([mine, jnp.broadcast_to(energy[None], (LINE, OWN, 128))], axis=2)
    loaded = exchanged(loaded, Y)
    force_rows = jnp.sum(loaded[:, :, :WIDTH], axis=0)
    energy = jnp.sum(loaded[:, 0, WIDTH:], axis=0)
    return (force_rows, energy[0])


def solution(mesh):
    fine = Mesh(mesh.devices.reshape(tuple(SIZES.values())), AXES)
    placed = P(AXES, None)
    return jax.shard_map(body, mesh=fine, in_specs=(placed, placed), out_specs=(placed, P()), check_vma=False)
```

```python
import jax
import jax.numpy as jnp
from jax import lax
from jax.experimental import pallas as pl
from jax.experimental.pallas import tpu as pltpu
from jax.sharding import Mesh, PartitionSpec as P

AXES = ("x", "yh", "zh", "zl", "yl", "c")
SIZES = dict(zip(AXES, (4, 4, 4, 2, 2, 2)))
Y = ("yh", "yl")
Z = ("zh", "zl")
OWN = 16
WIDTH = 1024
LINE = 8
UNITS = 16
COUNT = LINE * 2 * OWN
DEPTH = UNITS * OWN
ROOT_WIDTH = 32.0
TOTAL = 8192.0
NT = (((1,), (1,)), ((), ()))
NN = (((1,), (0,)), ((), ()))
SMEM = pl.BlockSpec(memory_space=pltpu.SMEM)
VMEM = pl.BlockSpec(memory_space=pltpu.VMEM)
PARAMS = pltpu.CompilerParams(vmem_limit_bytes=28 * 1024 * 1024)


def shape(*dims, dtype=jnp.float32):
    return jax.ShapeDtypeStruct(dims, dtype)


def cost(flops):
    return pl.CostEstimate(flops=flops, bytes_accessed=4_000_000, transcendentals=200_000)


def halves(value):
    high = value.astype(jnp.bfloat16)
    low = (value - high.astype(jnp.float32)).astype(jnp.bfloat16)
    return high, low


def product(left, right, dims):
    (left_at,), (right_at,) = dims[0]
    left = jnp.concatenate([left[0], left[0], left[1]], axis=left_at)
    right = jnp.concatenate([right[0], right[1], right[0]], axis=right_at)
    return lax.dot_general(left, right, dims, preferred_element_type=jnp.float32)


def flat(block):
    return block.reshape(block.shape[0] * block.shape[1], block.shape[2])


def sign(kind):
    return -1.0 if kind == 0 else 1.0


def pair_kernel(place_ref, first_ref, second_ref, cols_ref, *refs):
    row_refs, (out_refs, energy_ref) = (first_ref, second_ref), refs[-2:]
    before = refs[0][0:1, 0:1] if len(refs) == 3 else 0.0

    def rows_of(kind):
        return jnp.concatenate([flat(ref[:, kind * OWN : (kind + 1) * OWN, :]) for ref in row_refs], axis=0)

    row_gen = rows_of(0)
    rows = jnp.concatenate([row_gen, rows_of(1)], axis=0)
    rows_sq = jnp.sum(rows * rows, axis=1, keepdims=True)
    rows_hl = halves(rows)
    total = jnp.zeros((COUNT, 1), jnp.float32)
    energy = jnp.zeros((1, DEPTH), jnp.float32)
    force = jnp.zeros((COUNT, WIDTH), jnp.float32)
    for kind in range(2):
        cols = flat(cols_ref[:, kind * OWN : (kind + 1) * OWN, :])
        cols_sq = jnp.sum(cols * cols, axis=1, keepdims=True)
        cols_sq = jnp.transpose(jnp.broadcast_to(cols_sq, (DEPTH, 128)))[0:1, :]
        cols_hl = halves(cols)
        used = COUNT if kind == 0 else 2 * COUNT
        inner = product((rows_hl[0][:used], rows_hl[1][:used]), cols_hl, NT)
        square = jnp.maximum(rows_sq[:used] + cols_sq - 2.0 * inner, 0.0) + 1.0
        inverse = lax.rsqrt(square)
        distance = square * inverse
        near = jnp.sum(distance[:COUNT], axis=0, keepdims=True)
        if kind == 0:
            energy = energy - near
        else:
            energy = energy + (2.0 * near - jnp.sum(distance[COUNT:], axis=0, keepdims=True))
        weight = (sign(kind) * ROOT_WIDTH / TOTAL) * inverse[:COUNT]
        total = total + jnp.sum(weight, axis=1, keepdims=True)
        force = force + product(halves(weight), cols_hl, NN)
    force = total * row_gen - force
    for group in range(2):
        for member in range(LINE):
            at = (group * LINE + member) * OWN
            to = 2 * (member % 4) + place_ref[member // 4]
            out_refs[group, to, :, :WIDTH] = force[at : at + OWN]
    energy = before + jnp.sum(energy, axis=1, keepdims=True) / (TOTAL * TOTAL * ROOT_WIDTH)
    energy_ref[...] = jnp.broadcast_to(energy, energy_ref.shape)
    if out_refs.shape[-1] > WIDTH:
        out_refs[:, :, :, WIDTH:] = jnp.broadcast_to(energy, (*out_refs.shape[:3], 128))


def pairs(place, first, second, cols, *before, flops):
    extra = 128 * len(before)
    return pl.pallas_call(
        pair_kernel,
        out_shape=(shape(2, LINE, OWN, WIDTH + extra), shape(8, 128)),
        in_specs=[SMEM] + [VMEM] * (3 + len(before)),
        out_specs=[VMEM] * 2,
        compiler_params=PARAMS,
        cost_estimate=cost(flops),
    )(place, first, second, cols, *before)


def spread_kernel(gen_ref, data_ref, own_ref, copies_ref):
    own_ref[:OWN], own_ref[OWN:] = gen_ref[...], data_ref[...]
    for peer in range(4):
        copies_ref[peer, :OWN], copies_ref[peer, OWN:] = gen_ref[...], data_ref[...]


def spread(generated, data):
    return pl.pallas_call(
        spread_kernel,
        out_shape=(shape(2 * OWN, WIDTH), shape(4, 2 * OWN, WIDTH)),
        in_specs=[VMEM] * 2,
        out_specs=[VMEM] * 2,
    )(generated, data)


def sent(value, axes, move):
    sizes = [SIZES[a] for a in axes]
    perm = []
    total = 1
    for s in sizes:
        total *= s
    for source in range(total):
        rest, place = source, []
        for s in reversed(sizes):
            place.insert(0, rest % s)
            rest //= s
        target = 0
        for s, p in zip(sizes, move(*place)):
            target = target * s + p % s
        perm.append((source, target))
    return lax.ppermute(value, axes, perm)


def exchanged(value, axes):
    return lax.all_to_all(value, axes, split_axis=0, concat_axis=0, tiled=True)


def swapped(value):
    return sent(value, ("c",), lambda c: (1 - c,))


def along(value, axes, steps):
    return sent(value, axes, lambda high, low: divmod((2 * high + low + steps) % 8, 2))


def shifted(value, axes, steps):
    def move(high, low, c):
        return (*divmod((2 * high + low + steps * (1 - 2 * c)) % 8, 2), c)

    return sent(value, (*axes, "c"), move)


def joined(*parts):
    return jnp.concatenate(parts, axis=0)


def body(generated, data):
    own, copies = spread(generated, data)
    line = exchanged(copies, ("yh",))
    parity = jnp.stack([own] + [along(own, Z, steps) for steps in (2, -2, 4)])
    parity, _ = lax.optimization_barrier((parity, line))
    cols = exchanged(jnp.broadcast_to(parity[None], (4,) + parity.shape), ("x",))
    line = joined(line, shifted(line, Y, -1))
    near = shifted(line, Z, -1)
    line_away = swapped(line)
    cols, near = lax.optimization_barrier((cols.reshape((UNITS,) + own.shape), near))
    near_away = swapped(near)
    yl = lax.axis_index("yl")
    place = jnp.stack([yl, 1 - yl]).astype(jnp.int32)
    mine, energy = pairs(place, line, near, cols, flops=6_000_000_000)
    back, energy = pairs(place, line_away, near_away, cols, energy, flops=2_000_000_000)
    back = swapped(back)
    energy = energy[:1] + back[0, 0, :1, WIDTH:]
    back = back[:, :, :, :WIDTH]
    mine, away = mine[0], mine[1]
    energy = jnp.sum(exchanged(jnp.broadcast_to(energy[None], (32, 1, 128)), ("x", "zh", "zl")), axis=0)
    mine = mine + back[0] + shifted(away + back[1], Z, 1)
    loaded = jnp.concatenate([mine, jnp.broadcast_to(energy[None], (LINE, OWN, 128))], axis=2)
    loaded = exchanged(loaded, Y)
    force_rows = jnp.sum(loaded[:, :, :WIDTH], axis=0)
    energy = jnp.sum(loaded[:, 0, WIDTH:], axis=0)
    return (force_rows, energy[0])


def solution(mesh):
    fine = Mesh(mesh.devices.reshape(tuple(SIZES.values())), AXES)
    placed = P(AXES, None)
    return jax.shard_map(body, mesh=fine, in_specs=(placed, placed), out_specs=(placed, P()), check_vma=False)
```

```python
import jax
import jax.numpy as jnp
from jax import lax
from jax.experimental import pallas as pl
from jax.experimental.pallas import tpu as pltpu
from jax.sharding import Mesh, PartitionSpec as P

AXES = ("x", "yh", "zh", "zl", "yl", "c")
SIZES = dict(zip(AXES, (4, 4, 4, 2, 2, 2)))
Y = ("yh", "yl")
Z = ("zh", "zl")
OWN = 16
WIDTH = 1024
LINE = 8
UNITS = 16
COUNT = LINE * 2 * OWN
DEPTH = UNITS * OWN
ROOT_WIDTH = 32.0
TOTAL = 8192.0
NT = (((1,), (1,)), ((), ()))
NN = (((1,), (0,)), ((), ()))
SMEM = pl.BlockSpec(memory_space=pltpu.SMEM)
VMEM = pl.BlockSpec(memory_space=pltpu.VMEM)
PARAMS = pltpu.CompilerParams(vmem_limit_bytes=28 * 1024 * 1024)


def shape(*dims, dtype=jnp.float32):
    return jax.ShapeDtypeStruct(dims, dtype)


def cost(flops):
    return pl.CostEstimate(flops=flops, bytes_accessed=4_000_000, transcendentals=200_000)


def halves(value):
    high = value.astype(jnp.bfloat16)
    low = (value - high.astype(jnp.float32)).astype(jnp.bfloat16)
    return high, low


def product(left, right, dims):
    def dot(a, b):
        return lax.dot_general(a, b, dims, preferred_element_type=jnp.float32)

    return dot(left[0], right[0]) + (dot(left[0], right[1]) + dot(left[1], right[0]))


def flat(block):
    return block.reshape(block.shape[0] * block.shape[1], block.shape[2])


def sign(kind):
    return -1.0 if kind == 0 else 1.0


def pair_kernel(place_ref, first_ref, second_ref, cols_ref, *refs):
    row_refs, (out_refs, energy_ref) = (first_ref, second_ref), refs[-2:]
    before = refs[0][0:1, 0:1] if len(refs) == 3 else 0.0

    def rows_of(kind):
        return jnp.concatenate([flat(ref[:, kind * OWN : (kind + 1) * OWN, :]) for ref in row_refs], axis=0)

    row_gen = rows_of(0)
    rows = jnp.concatenate([row_gen, rows_of(1)], axis=0)
    rows_sq = jnp.sum(rows * rows, axis=1, keepdims=True)
    rows_hl = halves(rows)
    total = jnp.zeros((COUNT, 1), jnp.float32)
    energy = jnp.zeros((1, DEPTH), jnp.float32)
    force = jnp.zeros((COUNT, WIDTH), jnp.float32)
    for kind in range(2):
        cols = flat(cols_ref[:, kind * OWN : (kind + 1) * OWN, :])
        cols_sq = jnp.sum(cols * cols, axis=1, keepdims=True)
        cols_sq = jnp.transpose(jnp.broadcast_to(cols_sq, (DEPTH, 128)))[0:1, :]
        cols_hl = halves(cols)
        used = COUNT if kind == 0 else 2 * COUNT
        inner = product((rows_hl[0][:used], rows_hl[1][:used]), cols_hl, NT)
        square = jnp.maximum(rows_sq[:used] + cols_sq - 2.0 * inner, 0.0) + 1.0
        inverse = lax.rsqrt(square)
        distance = square * inverse
        near = jnp.sum(distance[:COUNT], axis=0, keepdims=True)
        if kind == 0:
            energy = energy - near
        else:
            energy = energy + (2.0 * near - jnp.sum(distance[COUNT:], axis=0, keepdims=True))
        weight = (sign(kind) * ROOT_WIDTH / TOTAL) * inverse[:COUNT]
        total = total + jnp.sum(weight, axis=1, keepdims=True)
        force = force + product(halves(weight), cols_hl, NN)
    force = total * row_gen - force
    for group in range(2):
        for member in range(LINE):
            at = (group * LINE + member) * OWN
            to = 2 * (member % 4) + place_ref[member // 4]
            out_refs[group, to, :, :WIDTH] = force[at : at + OWN]
    energy = before + jnp.sum(energy, axis=1, keepdims=True) / (TOTAL * TOTAL * ROOT_WIDTH)
    energy_ref[...] = jnp.broadcast_to(energy, energy_ref.shape)
    if out_refs.shape[-1] > WIDTH:
        out_refs[:, :, :, WIDTH:] = jnp.broadcast_to(energy, (*out_refs.shape[:3], 128))


def pairs(place, first, second, cols, *before, flops):
    extra = 128 * len(before)
    return pl.pallas_call(
        pair_kernel,
        out_shape=(shape(2, LINE, OWN, WIDTH + extra), shape(8, 128)),
        in_specs=[SMEM] + [VMEM] * (3 + len(before)),
        out_specs=[VMEM] * 2,
        compiler_params=PARAMS,
        cost_estimate=cost(flops),
    )(place, first, second, cols, *before)


def spread_kernel(gen_ref, data_ref, own_ref, copies_ref):
    own_ref[:OWN], own_ref[OWN:] = gen_ref[...], data_ref[...]
    for peer in range(4):
        copies_ref[peer, :OWN], copies_ref[peer, OWN:] = gen_ref[...], data_ref[...]


def spread(generated, data):
    return pl.pallas_call(
        spread_kernel,
        out_shape=(shape(2 * OWN, WIDTH), shape(4, 2 * OWN, WIDTH)),
        in_specs=[VMEM] * 2,
        out_specs=[VMEM] * 2,
    )(generated, data)


def sent(value, axes, move):
    sizes = [SIZES[a] for a in axes]
    perm = []
    total = 1
    for s in sizes:
        total *= s
    for source in range(total):
        rest, place = source, []
        for s in reversed(sizes):
            place.insert(0, rest % s)
            rest //= s
        target = 0
        for s, p in zip(sizes, move(*place)):
            target = target * s + p % s
        perm.append((source, target))
    return lax.ppermute(value, axes, perm)


def exchanged(value, axes):
    return lax.all_to_all(value, axes, split_axis=0, concat_axis=0, tiled=True)


def swapped(value):
    return sent(value, ("c",), lambda c: (1 - c,))


def along(value, axes, steps):
    return sent(value, axes, lambda high, low: divmod((2 * high + low + steps) % 8, 2))


def shifted(value, axes, steps):
    def move(high, low, c):
        return (*divmod((2 * high + low + steps * (1 - 2 * c)) % 8, 2), c)

    return sent(value, (*axes, "c"), move)


def joined(*parts):
    return jnp.concatenate(parts, axis=0)


def body(generated, data):
    own, copies = spread(generated, data)
    line = exchanged(copies, ("yh",))
    parity = [own] + [along(own, Z, steps) for steps in (2, -2, 4)]
    parity = joined(*parity * 4).reshape((4, 4) + own.shape)
    parity, _ = lax.optimization_barrier((parity, line))
    cols = exchanged(parity, ("x",))
    line = joined(line, shifted(line, Y, -1))
    near = shifted(line, Z, -1)
    line_away = swapped(line)
    cols, near = lax.optimization_barrier((cols.reshape((UNITS,) + own.shape), near))
    near_away = swapped(near)
    yl = lax.axis_index("yl")
    place = jnp.stack([yl, 1 - yl]).astype(jnp.int32)
    mine, energy = pairs(place, line, near, cols, flops=6_000_000_000)
    back, energy = pairs(place, line_away, near_away, cols, energy, flops=2_000_000_000)
    back = swapped(back)
    energy = energy[:1] + back[0, 0, :1, WIDTH:]
    back = back[:, :, :, :WIDTH]
    mine, away = mine[0], mine[1]
    energy = jnp.sum(exchanged(jnp.broadcast_to(energy[None], (32, 1, 128)), ("x", "zh", "zl")), axis=0)
    mine = mine + back[0] + shifted(away + back[1], Z, 1)
    loaded = jnp.concatenate([mine, jnp.broadcast_to(energy[None], (LINE, OWN, 128))], axis=2)
    loaded = exchanged(loaded, Y)
    force_rows = jnp.sum(loaded[:, :, :WIDTH], axis=0)
    energy = jnp.sum(loaded[:, 0, WIDTH:], axis=0)
    return (force_rows, energy[0])


def solution(mesh):
    fine = Mesh(mesh.devices.reshape(tuple(SIZES.values())), AXES)
    placed = P(AXES, None)
    return jax.shard_map(body, mesh=fine, in_specs=(placed, placed), out_specs=(placed, P()), check_vma=False)
```
